32 devices in a mesh: seq: 8 (over z, x), dp: 4 (over y, core).
Axes of the slice: x: 2, y: 2, z: 4, core: 2. Of those that a mesh axis runs over, the one named last changes fastest.
Arguments:
- linear_queries: bfloat16 [4, 1024, 2048], P('dp', 'seq'), may hold values from -6 to 6
- linear_keys: bfloat16 [4, 1024, 2048], P('dp', 'seq'), may hold values from -6 to 6
- window_queries: bfloat16 [4, 1024, 2048], P('dp', 'seq'), may hold values from -41 to 41
- window_keys: bfloat16 [4, 1024, 2048], P('dp', 'seq'), may hold values from -12 to 12
- values: bfloat16 [4, 1024, 2048], P('dp', 'seq'), may hold values from -8 to 8
- cotangent: bfloat16 [4, 1024, 2048], P('dp', 'seq'), may hold values from -10 to 10
- feature_map: bfloat16 [16, 128, 128], replicated, may hold values from -0.5 to 0.5
Outputs:
- attended: bfloat16 [4, 1024, 2048], P('dp', 'seq')
- dlinear_queries: bfloat16 [4, 1024, 2048], P('dp', 'seq')
- dlinear_keys: bfloat16 [4, 1024, 2048], P('dp', 'seq')
- dwindow_queries: bfloat16 [4, 1024, 2048], P('dp', 'seq')
- dwindow_keys: bfloat16 [4, 1024, 2048], P('dp', 'seq')
- dvalues: bfloat16 [4, 1024, 2048], P('dp', 'seq')
- dfeature_map: float32 [16, 128, 128], replicated
The draws below stay inside these ranges and needn't reach their ends.
All inputs are finite; a program needn't handle non-finite values.
Results may differ from the reference program's by a relative error of at most 0.009.
Values may be sent and summed in bfloat16 or wider, within the bound.
No kernel may reach another device: no remote copies, remote signals or barrier semaphores. Data moves between devices by JAX's collectives and lax.ppermute only.
A program may use at most 192 MiB of HBM per device.

```python
import jax
import jax.numpy as jnp
from jax import lax

HEADS = 16
HD = 128
WINDOW = 64
WIDTH = 2048
LEN = 1024
SEQS = 4


def window_pair(key):
    shape = (SEQS, LEN, HEADS * HD)
    queries = jnp.clip(jax.random.normal(jax.random.fold_in(key, 101), shape, jnp.float32), -4.0, 4.0)
    keyrows = jnp.clip(jax.random.normal(jax.random.fold_in(key, 102), shape, jnp.float32), -4.0, 4.0)
    return (queries, keyrows)


def draw_window_queries(key, part):
    return window_pair(key)[0].astype(jnp.bfloat16)


def draw_window_keys(key, part):
    return window_pair(key)[1].astype(jnp.bfloat16)


def draw_values(key, part):
    shape = (SEQS, LEN, HEADS * HD)
    noise = jnp.clip(jax.random.normal(jax.random.fold_in(key, 201), shape, jnp.float32), -4.0, 4.0)
    center = jnp.clip(jax.random.normal(jax.random.fold_in(key, 202), (SEQS, 1, HEADS * HD), jnp.float32), -3.0, 3.0)
    segment = jnp.arange(LEN, dtype=jnp.int32) * 8 // LEN
    offsets = jnp.clip(1.2 * jax.random.normal(jax.random.fold_in(key, 203), (SEQS, 8, HEADS * HD), jnp.float32), -3.6, 3.6)
    drift = jnp.take(offsets, segment, axis=1)
    return jnp.clip(noise + center + drift, -8.0, 8.0).astype(jnp.bfloat16)


def draw_cotangent(key, part):
    shape = (SEQS, LEN, HEADS * HD)
    noise = jnp.clip(jax.random.normal(jax.random.fold_in(key, 301), shape, jnp.float32), -4.0, 4.0)
    common = 0.7 * jax.random.normal(jax.random.fold_in(key, 302), (SEQS, 1, HEADS * HD), jnp.float32)
    return jnp.clip(2.0 * (noise + common), -10.0, 10.0).astype(jnp.bfloat16)


def levels(rng, extent, shards, low, high):
    level, own = 1.0, jax.random.fold_in(rng, 6)
    for position, blocks in shards:
        draws = jnp.exp(jax.random.uniform(jax.random.fold_in(own, position), (blocks,), jnp.float32, low / len(shards), high / len(shards)))
        level = level * jnp.repeat(draws, extent[position] // blocks).reshape([-1 if axis == position else 1 for axis in range(len(extent))])
    return level


def scatter_about(key, shape, scale, limit, pieces=(), kind=jnp.bfloat16):
    gain = levels(key, shape, pieces, -0.22, 0.18) if pieces else 1.0
    result = jax.random.normal(key, shape, jnp.float32) * scale * gain
    return jnp.minimum(jnp.maximum(result, -limit), limit).astype(kind)


def setup_inputs(seed: int = 0) -> dict:
    key_of = jax.random.split(jax.random.key(seed), 8)
    linear_queries = scatter_about(key_of[0], (SEQS, LEN, WIDTH), 1.0, 6.0, ((0, 4), (1, 8)))
    linear_keys = scatter_about(key_of[1], (SEQS, LEN, WIDTH), 1.0, 6.0, ((0, 4), (1, 8)))
    window_queries = draw_window_queries(jax.random.fold_in(key_of[7], 71), 0)
    window_keys = draw_window_keys(jax.random.fold_in(key_of[7], 71), 0)
    values = draw_values(jax.random.fold_in(key_of[7], 71), 0)
    cotangent = draw_cotangent(jax.random.fold_in(key_of[7], 71), 0)
    feature_map = scatter_about(key_of[6], (HEADS, HD, HD), HD ** -0.5, 0.5)
    return {"linear_queries": linear_queries, "linear_keys": linear_keys, "window_queries": window_queries, "window_keys": window_keys, "values": values, "cotangent": cotangent, "feature_map": feature_map}


def highest(form, left, right):
    return jnp.einsum(form, left.astype(jnp.float32), right.astype(jnp.float32), precision=lax.Precision.HIGHEST)


def feature(inputs, feature_map):
    before = highest('htd,hde->hte', inputs, feature_map)
    mapped = jnp.where(before > 0, before + 1.0, jnp.exp(jnp.minimum(before, 0.0)))
    return before, mapped.astype(jnp.bfloat16)


def slope(before):
    return jnp.where(before > 0, 1.0, jnp.exp(jnp.minimum(before, 0.0)))


def split_heads(matrix):
    return matrix.reshape(matrix.shape[0], HEADS, HD).transpose(1, 0, 2)


def join_heads(tensor):
    return tensor.transpose(1, 0, 2).reshape(tensor.shape[1], HEADS * HD)


def exclusive(terms, reverse):
    zero = jnp.zeros_like(terms[:1])
    if reverse:
        totals = jnp.flip(jnp.cumsum(jnp.flip(terms, 0), axis=0), 0)
        return jnp.concatenate([totals[1:], zero], axis=0)
    totals = jnp.cumsum(terms, axis=0)
    return jnp.concatenate([zero, totals[:-1]], axis=0)


def band_mask():
    rows = lax.broadcasted_iota(jnp.int32, (WINDOW, 2 * WINDOW), 0)
    cols = lax.broadcasted_iota(jnp.int32, (WINDOW, 2 * WINDOW), 1)
    offset = cols - rows
    return (offset >= 1) & (offset <= WINDOW)


def window_mask(blocks, start):
    cols = lax.broadcasted_iota(jnp.int32, (blocks, WINDOW, 2 * WINDOW), 2)
    block = lax.broadcasted_iota(jnp.int32, (blocks, WINDOW, 2 * WINDOW), 0)
    keypos = start + block * WINDOW + cols - WINDOW
    return band_mask()[None] & (keypos >= 0)


def causal_mask():
    rows = lax.broadcasted_iota(jnp.int32, (WINDOW, WINDOW), 0)
    cols = lax.broadcasted_iota(jnp.int32, (WINDOW, WINDOW), 1)
    return rows >= cols


def pairs(rim, inputs):
    blocks = inputs.shape[1] // WINDOW
    early = jnp.concatenate([rim, inputs[:, :inputs.shape[1] - WINDOW]], axis=1).reshape(HEADS, blocks, WINDOW, HD)
    late = inputs.reshape(HEADS, blocks, WINDOW, HD)
    return jnp.concatenate([early, late], axis=2)


def softmax_rows(score, mask):
    top = jnp.max(jnp.where(mask, score, -jnp.inf), axis=-1, keepdims=True)
    expo = jnp.exp(jnp.where(mask, score - top, -jnp.inf))
    return expo / jnp.sum(expo, axis=-1, keepdims=True)


def fold_pairs(pair, rim):
    after = jnp.concatenate([pair[:, 1:, :WINDOW], rim[:, None]], axis=1)
    return pair[:, :, WINDOW:] + after


def reference(linear_queries, linear_keys, window_queries, window_keys, values, cotangent, feature_map):
    def one_sequence(inputs):
        lin_query_rows, lin_key_rows, win_query_rows, win_key_rows, value_rows, grad_rows = inputs
        length = lin_query_rows.shape[0]
        blocks = length // WINDOW
        block_shape = (HEADS, blocks, WINDOW, HD)
        lin_scale = 1.0 / (HD * LEN)
        inverse_root = HD ** -0.5
        query_heads = split_heads(lin_query_rows)
        key_heads = split_heads(lin_key_rows)
        pre_query, feat_query = feature(query_heads, feature_map)
        pre_key, feat_key = feature(key_heads, feature_map)
        query_blocks = feat_query.reshape(block_shape)
        key_blocks = feat_key.reshape(block_shape)
        value_heads = split_heads(value_rows)
        value_blocks = value_heads.reshape(block_shape)
        causal = causal_mask()
        lin_scores = jnp.where(causal, highest('hncf,hnsf->hncs', query_blocks, key_blocks), 0.0)
        state_in = exclusive(highest('hnsf,hnsd->nhfd', key_blocks, value_blocks), False)
        lin = (highest('hncs,hnsd->hncd', lin_scores, value_blocks) + highest('hncf,nhfd->hncd', query_blocks, state_in)) * lin_scale
        rim = jnp.zeros((HEADS, WINDOW, HD), jnp.bfloat16)
        win_queries = split_heads(win_query_rows).reshape(block_shape)
        key_pairs = pairs(rim, split_heads(win_key_rows))
        value_pairs = pairs(rim, value_heads)
        mask = window_mask(blocks, 0)
        prob = softmax_rows(highest('hncd,hnsd->hncs', win_queries, key_pairs) * inverse_root, mask[None])
        prob_b = prob.astype(jnp.bfloat16)
        win = highest('hncs,hnsd->hncd', prob_b, value_pairs)
        attended = join_heads((lin + win).astype(jnp.bfloat16).reshape(HEADS, length, HD))
        grad_heads = split_heads(grad_rows).reshape(block_shape)
        grad_lin = grad_heads.astype(jnp.float32) * lin_scale
        mixed = jnp.where(causal, highest('hncd,hnsd->hncs', grad_lin, value_blocks), 0.0)
        dfeat_query = highest('hncs,hnsf->hncf', mixed, key_blocks) + highest('hncd,nhfd->hncf', grad_lin, state_in)
        state_after = exclusive(highest('hncf,hncd->nhfd', query_blocks, grad_lin), True)
        dfeat_key = highest('hncs,hncf->hnsf', mixed, query_blocks) + highest('nhfd,hnsd->hnsf', state_after, value_blocks)
        dvalue_lin = highest('hncs,hncd->hnsd', lin_scores, grad_lin) + highest('hnsf,nhfd->hnsd', key_blocks, state_after)
        dpre_query = (dfeat_query.reshape(HEADS, length, HD) * slope(pre_query)).astype(jnp.bfloat16)
        dpre_key = (dfeat_key.reshape(HEADS, length, HD) * slope(pre_key)).astype(jnp.bfloat16)
        dlin_queries = join_heads(highest('htf,hdf->htd', dpre_query, feature_map).astype(jnp.bfloat16))
        dlin_keys = join_heads(highest('htf,hdf->htd', dpre_key, feature_map).astype(jnp.bfloat16))
        map_terms = highest('htd,hte->hde', query_heads, dpre_query) + highest('htd,hte->hde', key_heads, dpre_key)
        dprob = highest('hncd,hnsd->hncs', grad_heads, value_pairs)
        delta = jnp.sum(prob * dprob, axis=-1, keepdims=True)
        dscore = (prob * (dprob - delta) * inverse_root).astype(jnp.bfloat16)
        dwin_queries = join_heads(highest('hncs,hnsd->hncd', dscore, key_pairs).reshape(HEADS, length, HD).astype(jnp.bfloat16))
        empty = jnp.zeros((HEADS, WINDOW, HD), jnp.float32)
        dkey_win = fold_pairs(highest('hncs,hncd->hnsd', dscore, win_queries), empty)
        dvalue_win = fold_pairs(highest('hncs,hncd->hnsd', prob_b, grad_heads), empty)
        dwin_keys = join_heads(dkey_win.reshape(HEADS, length, HD).astype(jnp.bfloat16))
        dvalue_all = join_heads((dvalue_lin + dvalue_win).reshape(HEADS, length, HD).astype(jnp.bfloat16))
        return attended, dlin_queries, dlin_keys, dwin_queries, dwin_keys, dvalue_all, map_terms

    results = lax.map(one_sequence, (linear_queries, linear_keys, window_queries, window_keys, values, cotangent))
    map_grad = jnp.sum(results[6], axis=0) * (SEQS * LEN) ** -0.5
    return results[0], results[1], results[2], results[3], results[4], results[5], map_grad
```

```python
import jax
import jax.numpy as jnp
from jax import lax
from jax.experimental import pallas as pl
from jax.experimental.pallas import tpu as pltpu
from jax.sharding import PartitionSpec as P

HEADS = 16
HD = 128
WINDOW = 64
HALF = HEADS // 2
GROUP = 4
LANES = GROUP * HD
BF = jnp.bfloat16
F32 = jnp.float32
WIDE = HEADS * HD


def dot(left, right):
    return jnp.dot(left, right, preferred_element_type=F32)


def dot_nt(left, right):
    return lax.dot_general(left, right, (((1,), (1,)), ((), ())), preferred_element_type=F32)


def dot_tn(left, right):
    return lax.dot_general(left, right, (((0,), (0,)), ((), ())), preferred_element_type=F32)


def phi(before):
    return jnp.where(before > 0, before + 1.0, jnp.exp(jnp.minimum(before, 0.0)))


def col(head):
    return slice(head * HD, (head + 1) * HD)


def feature_kernel(off, lq, lk, v, g, fm, *rest):
    fq_out, fk_out, t_out = rest[-3:]
    for h in range(GROUP):
        c = col(h)
        w = fm[h]
        fq = phi(dot(lq[:, c], w)).astype(BF)
        fk = phi(dot(lk[:, c], w)).astype(BF)
        fq_out[:, c] = fq
        fk_out[:, c] = fk
        t_out[h, 0] = dot_tn(fk, v[:, c]).astype(BF)
        t_out[h, 1] = dot_tn(fq, g[:, c]).astype(BF)


def cost(flops, moved):
    return pl.CostEstimate(flops=flops, bytes_accessed=moved, transcendentals=0)


def features(off, lq, lk, v, g, fm, earlier):
    tokens = lq.shape[0]
    cols = pl.BlockSpec((tokens, LANES), lambda i, o: (0, o[0] + i))
    maps = pl.BlockSpec((GROUP, HD, HD), lambda i, o: (o[0] + i, 0, 0))
    kept = pl.BlockSpec(memory_space=pl.ANY)
    row = jax.ShapeDtypeStruct((tokens, WIDE), BF)
    return pl.pallas_call(
        feature_kernel,
        grid_spec=pltpu.PrefetchScalarGridSpec(
            num_scalar_prefetch=1,
            grid=(HALF // GROUP,),
            in_specs=[cols] * 4 + [maps] + [kept] * len(earlier),
            out_specs=[cols, cols, pl.BlockSpec((GROUP, 2, HD, HD), lambda i, o: (i, 0, 0, 0))],
        ),
        out_shape=[row, row, jax.ShapeDtypeStruct((HALF, 2, HD, HD), BF)],
        input_output_aliases={6: 0, 7: 1} if earlier else {},
        cost_estimate=cost(2 * HALF * 4 * tokens * HD * HD, 4_000_000),
        compiler_params=pltpu.CompilerParams(vmem_limit_bytes=32 * 1024 * 1024),
        name="features",
    )(off, lq, lk, v, g, fm, *earlier)


def local_kernel(
    info, wq, wk, v, g, rim_k, rim_v, fq, fk,
    att, dv, dfq, dfk, dwq, dwk, tail_k, send_k, send_v,
):
    tokens = wq.shape[0]
    scale = jnp.float32(1.0 / HD) / info[1].astype(F32)
    root = HD ** (-0.5)
    rows = lax.broadcasted_iota(jnp.int32, (tokens, 2 * WINDOW), 0)
    cols = lax.broadcasted_iota(jnp.int32, (tokens, 2 * WINDOW), 1)
    offset = cols - rows % WINDOW
    absent = (info[0] == 0) & (rows < WINDOW) & (cols < WINDOW)
    band = (offset >= 1) & (offset <= WINDOW) & jnp.logical_not(absent)
    causal_r = lax.broadcasted_iota(jnp.int32, (tokens, tokens), 0)
    causal_c = lax.broadcasted_iota(jnp.int32, (tokens, tokens), 1)
    causal = causal_r >= causal_c
    for h in range(GROUP):
        c = col(h)
        q, k, val, grad = wq[:, c], wk[:, c], v[:, c], g[:, c]
        kp = jnp.concatenate([rim_k[:, c], k[:WINDOW]], axis=0)
        vp = jnp.concatenate([rim_v[:, c], val[:WINDOW]], axis=0)
        score = jnp.concatenate([dot_nt(q[:WINDOW], kp), dot_nt(q[WINDOW:], k)], axis=0) * root
        score = jnp.where(band, score, -jnp.inf)
        expo = jnp.exp(score - jnp.max(score, axis=-1, keepdims=True))
        prob = expo / jnp.sum(expo, axis=-1, keepdims=True)
        prob_b = prob.astype(BF)
        mixed = dot_nt(grad, val)
        dprob = jnp.concatenate([dot_nt(grad[:WINDOW], vp), mixed[WINDOW:]], axis=0)
        delta = jnp.sum(prob * dprob, axis=-1, keepdims=True)
        dscore = (prob * (dprob - delta) * root).astype(BF)
        win = jnp.concatenate([dot(prob_b[:WINDOW], vp), dot(prob_b[WINDOW:], val)], axis=0)
        dwq[:, c] = jnp.concatenate(
            [dot(dscore[:WINDOW], kp), dot(dscore[WINDOW:], k)], axis=0
        ).astype(BF)
        dk0 = dot_tn(dscore[:WINDOW], q[:WINDOW])
        dk1 = dot_tn(dscore[WINDOW:], q[WINDOW:])
        dv0 = dot_tn(prob_b[:WINDOW], grad[:WINDOW])
        dv1 = dot_tn(prob_b[WINDOW:], grad[WINDOW:])
        send_k[:, c] = dk0[:WINDOW].astype(BF)
        send_v[:, c] = dv0[:WINDOW].astype(BF)
        dwk[:, c] = jnp.concatenate([dk0[WINDOW:] + dk1[:WINDOW], dk1[WINDOW:]], axis=0).astype(BF)
        tail_k[:, c] = dk1[WINDOW:]
        dv_win = jnp.concatenate([dv0[WINDOW:] + dv1[:WINDOW], dv1[WINDOW:]], axis=0)
        q_feat, k_feat = fq[:, c], fk[:, c]
        scores = jnp.where(causal, dot_nt(q_feat, k_feat), 0.0).astype(BF)
        mixed = jnp.where(causal, mixed, 0.0).astype(BF)
        att[:, c] = dot(scores, val) * scale + win
        dv[:, c] = dot_tn(scores, grad) * scale + dv_win
        dfq[:, c] = dot(mixed, k_feat)
        dfk[:, c] = dot_tn(mixed, q_feat)


def local_part(info, wq, wk, v, g, rim_k, rim_v, fq, fk):
    tokens = wq.shape[0]
    cols = pl.BlockSpec((tokens, LANES), lambda i, o: (0, i))
    rims = pl.BlockSpec((WINDOW, LANES), lambda i, o: (0, i))
    wide = jax.ShapeDtypeStruct((tokens, WIDE), F32)
    narrow = jax.ShapeDtypeStruct((tokens, WIDE), BF)
    rim = jax.ShapeDtypeStruct((WINDOW, WIDE), BF)
    return pl.pallas_call(
        local_kernel,
        grid_spec=pltpu.PrefetchScalarGridSpec(
            num_scalar_prefetch=1,
            grid=(HEADS // GROUP,),
            in_specs=[cols] * 4 + [rims] * 2 + [cols] * 2,
            out_specs=[cols] * 6 + [rims] * 3,
        ),
        out_shape=[wide] * 4 + [narrow] * 2 + [jax.ShapeDtypeStruct((WINDOW, WIDE), F32), rim, rim],
        cost_estimate=cost(2 * HEADS * 15 * tokens * HD * HD, 10_000_000),
        compiler_params=pltpu.CompilerParams(vmem_limit_bytes=32 * 1024 * 1024),
        name="local_part",
    )(info, wq, wk, v, g, rim_k, rim_v, fq, fk)


def state_kernel(off, lq, lk, v, g, fm, fq, fk, state, att_p, dv_p, dfq_p, dfk_p, *rest):
    att, dlq, dlk, dv, tail_v, dmap = rest[-6:]
    scale = jnp.float32(1.0 / HD) / off[1].astype(F32)
    for h in range(GROUP):
        c = col(h)
        before, after = state[h, 0], state[h, 1]
        w = fm[h]
        q_feat, k_feat, val, grad = fq[:, c], fk[:, c], v[:, c], g[:, c]
        dfq = (dfq_p[:, c] + dot_nt(grad, before)) * scale
        dfk = (dfk_p[:, c] + dot_nt(val, after)) * scale
        dpq = (dfq * jnp.minimum(q_feat.astype(F32), 1.0)).astype(BF)
        dpk = (dfk * jnp.minimum(k_feat.astype(F32), 1.0)).astype(BF)
        dmap[h] = (dot_tn(lq[:, c], dpq) + dot_tn(lk[:, c], dpk)).astype(BF)
        dlq[:, c] = dot_nt(dpq, w).astype(BF)
        dlk[:, c] = dot_nt(dpk, w).astype(BF)
        att[:, c] = (att_p[:, c] + dot(q_feat, before) * scale).astype(BF)
        grad_v = dv_p[:, c] + dot(k_feat, after) * scale
        dv[:, c] = grad_v.astype(BF)
        tail_v[:, c] = grad_v[WINDOW:]


def state_part(off, lq, lk, v, g, fm, fq, fk, state, parts, earlier):
    tokens = lq.shape[0]
    cols = pl.BlockSpec((tokens, LANES), lambda i, o: (0, o[0] + i))
    tails = pl.BlockSpec((WINDOW, LANES), lambda i, o: (0, o[0] + i))
    maps = pl.BlockSpec((GROUP, HD, HD), lambda i, o: (o[0] + i, 0, 0))
    own = pl.BlockSpec((GROUP, HD, HD), lambda i, o: (i, 0, 0))
    states = pl.BlockSpec((GROUP, 2, HD, HD), lambda i, o: (i, 0, 0, 0))
    kept = pl.BlockSpec(memory_space=pl.ANY)
    narrow = jax.ShapeDtypeStruct((tokens, WIDE), BF)
    return pl.pallas_call(
        state_kernel,
        grid_spec=pltpu.PrefetchScalarGridSpec(
            num_scalar_prefetch=1,
            grid=(HALF // GROUP,),
            in_specs=[cols] * 4 + [maps] + [cols] * 2 + [states] + [cols] * 4 + [kept] * len(earlier),
            out_specs=[cols] * 4 + [tails, own],
        ),
        out_shape=[narrow] * 4
        + [
            jax.ShapeDtypeStruct((WINDOW, WIDE), F32),
            jax.ShapeDtypeStruct((HALF, HD, HD), BF),
        ],
        input_output_aliases={13 + i: i for i in range(5)} if earlier else {},
        cost_estimate=cost(2 * HALF * 8 * tokens * HD * HD, 8_000_000),
        compiler_params=pltpu.CompilerParams(vmem_limit_bytes=32 * 1024 * 1024),
        name="state_part",
    )(off, lq, lk, v, g, fm, fq, fk, state, *parts, *earlier)


def finish_kernel(tail_k, rim_k, tail_v, rim_v, k_in, v_in, dk, dv):
    dk[...] = (tail_k[...] + rim_k[...].astype(F32)).astype(BF)
    dv[...] = (tail_v[...] + rim_v[...].astype(F32)).astype(BF)


def finish(tail_k, rim_k, tail_v, rim_v, dwk, dv):
    rims = pl.BlockSpec((WINDOW, WIDE), lambda i: (0, 0))
    last = pl.BlockSpec((WINDOW, WIDE), lambda i: (dwk.shape[0] // WINDOW - 1, 0))
    kept = pl.BlockSpec(memory_space=pl.ANY)
    row = jax.ShapeDtypeStruct(dwk.shape, BF)
    return pl.pallas_call(
        finish_kernel,
        grid=(1,),
        in_specs=[rims] * 4 + [kept] * 2,
        out_specs=[last, last],
        out_shape=[row, row],
        input_output_aliases={4: 0, 5: 1},
        cost_estimate=cost(1_000_000, 2_500_000),
        compiler_params=pltpu.CompilerParams(vmem_limit_bytes=32 * 1024 * 1024),
        name="finish",
    )(tail_k, rim_k, tail_v, rim_v, dwk, dv)


def flipped(block, bit):
    count = lax.axis_size("seq")
    return lax.ppermute(block, "seq", [(i, i ^ bit) for i in range(count)])


def flat_flipped(block, seq_bits, dp_bits):
    rows, width = lax.axis_size("seq"), lax.axis_size("dp")
    route = [
        (s * width + d, (s ^ seq_bits) * width + (d ^ dp_bits))
        for s in range(rows)
        for d in range(width)
    ]
    return lax.ppermute(block, ("seq", "dp"), route)


def passed_along(block, distance):
    devices = range(lax.axis_size("seq"))
    route = [(i - distance, i) for i in devices if i - distance in devices]
    return lax.ppermute(block, "seq", route)


def spread(block, level):
    count = lax.axis_size("seq")
    size = 2 << level
    total = None
    for turn in range(1 << level):
        route = []
        for base in range(0, count // 2, size):
            low, high = base + size // 2 - 1, base + size // 2
            for parity in range(2):
                route.append((2 * low + parity, 2 * (high + turn) + parity))
                route.append((2 * high + parity, 2 * (low - turn) + parity))
        came = lax.ppermute(block, "seq", route)
        total = came if total is None else total + came
    return total


def states(kept, came, place):
    odd = place % 2
    level_count = (lax.axis_size("seq") // 2).bit_length() - 1
    kept, came = kept.astype(F32), came.astype(F32)
    pair = kept + came
    low = jnp.zeros_like(pair[:, 0])
    high = jnp.zeros_like(low)
    for level in range(level_count):
        upper = ((place // 2) >> level) % 2 == 1
        send = jnp.where(upper, pair[:, 1] + high, pair[:, 0] + low).astype(BF)
        got = spread(send, level).astype(F32)
        low = low + jnp.where(upper, got, 0.0)
        high = high + jnp.where(upper, 0.0, got)
    first = odd == 0
    mine = jnp.stack(
        [low + jnp.where(first, 0.0, came[:, 0]), high + jnp.where(first, came[:, 1], 0.0)], axis=1
    )
    others = jnp.stack(
        [low + jnp.where(first, kept[:, 0], 0.0), high + jnp.where(first, 0.0, kept[:, 1])], axis=1
    )
    return mine.astype(BF), others.astype(BF)


def half_of(block, which):
    size = block.shape[0] // 2
    return lax.dynamic_slice_in_dim(block, which * size, size, 0)


def joined(own, other, which):
    return jnp.where(
        which == 0, jnp.concatenate([own, other], 0), jnp.concatenate([other, own], 0)
    )


def map_sum(own, other, odd, total_tokens):
    core = lax.axis_index("dp") % 2
    far = lax.axis_index("dp") // 2
    own, other = own.reshape(2, 2, 2, HD, HD), other.reshape(2, 2, 2, HD, HD)

    def at(block, index):
        return lax.dynamic_index_in_dim(block, index, 0, False)

    both = jnp.stack([own, other], axis=1)
    swapped = flat_flipped(at(both, 1 - core), 0, 1)
    mine = (at(both, core).astype(F32) + swapped.astype(F32)).astype(BF)
    near, beyond = mine[0], mine[1]
    a = flat_flipped(at(beyond, far), 1, 0)
    b = flat_flipped(at(near, 1 - far), 0, 2)
    c = flat_flipped(at(beyond, 1 - far), 1, 2)
    total = at(near, far).astype(F32) + a.astype(F32) + b.astype(F32) + c.astype(F32)
    bit = 2
    while bit < lax.axis_size("seq"):
        sent = total.astype(BF)
        total = sent.astype(F32) + flat_flipped(sent, bit, 0).astype(F32)
        bit *= 2
    done = total.astype(BF)
    a = flat_flipped(done, 1, 0)
    b = flat_flipped(done, 0, 2)
    c = flat_flipped(done, 1, 2)
    quarter = jnp.stack([joined(done[None], b[None], far), joined(a[None], c[None], far)], axis=0)
    swapped = flat_flipped(quarter, 0, 1)
    halves = jnp.where(core == 0, jnp.stack([quarter, swapped], 1), jnp.stack([swapped, quarter], 1))
    whole = jnp.where(odd == 0, halves, halves[::-1])
    return whole.reshape(HEADS, HD, HD).astype(F32) * total_tokens ** (-0.5)


def on_device(
    linear_queries, linear_keys, window_queries, window_keys, values, cotangent, feature_map
):
    tokens = linear_queries.shape[1]
    length = tokens * lax.axis_size("seq")
    total_tokens = length * lax.axis_size("dp") * linear_queries.shape[0]
    place = lax.axis_index("seq")
    odd = place % 2
    lq, lk, wq, wk, v, g = (
        x[0]
        for x in (linear_queries, linear_keys, window_queries, window_keys, values, cotangent)
    )
    steps = HALF // GROUP
    scalar = jnp.int32(length)
    own = jnp.stack([odd * steps, scalar]).astype(jnp.int32)
    other = jnp.stack([(1 - odd) * steps, scalar]).astype(jnp.int32)
    fq, fk, sums_other = features(other, lq, lk, v, g, feature_map, ())
    came = flipped(sums_other, 1)
    fq, fk, sums_own = features(own, lq, lk, v, g, feature_map, (fq, fk))
    came, tail_in = lax.optimization_barrier(
        (came, (wk[tokens - WINDOW :], v[tokens - WINDOW :]))
    )
    rim_k, rim_v = (passed_along(x, 1) for x in tail_in)
    info = jnp.stack([place, scalar]).astype(jnp.int32)
    local = local_part(info, wq, wk, v, g, rim_k, rim_v, fq, fk)
    att_p, dv_p, dfq_p, dfk_p, dwq, dwk, tail_k, send_k, send_v = local
    parts = (att_p, dv_p, dfq_p, dfk_p)
    mine, others = states(sums_own, came, place)
    state_other = flipped(others, 1)
    outs = state_part(own, lq, lk, v, g, feature_map, fq, fk, mine, parts, ())
    state_other, sends = lax.optimization_barrier((state_other, (send_k, send_v)))
    back_k, back_v = (passed_along(x, -1) for x in sends)
    map_own = outs[5]
    outs = state_part(other, lq, lk, v, g, feature_map, fq, fk, state_other, parts, outs[:5])
    attended, dlq, dlk, dv, tail_v, map_other = outs
    map_grad = map_sum(map_own, map_other, odd, total_tokens)
    dwk, dv = finish(tail_k, back_k, tail_v, back_v, dwk, dv)
    return attended[None], dlq[None], dlk[None], dwq[None], dwk[None], dv[None], map_grad


def solution(mesh):
    row = P("dp", "seq", None)
    return jax.shard_map(
        on_device,
        mesh=mesh,
        in_specs=(row,) * 6 + (P(),),
        out_specs=(row,) * 6 + (P(),),
        check_vma=False,
    )
```

```python
import functools

import jax
import jax.numpy as jnp
from jax import lax
from jax.experimental import pallas as pl
from jax.experimental.pallas import tpu as pltpu
from jax.sharding import PartitionSpec as P

HEADS = 16
HD = 128
WINDOW = 64
HALF = HEADS // 2
CHUNKS = 2
CHUNK = HALF // CHUNKS
GROUP = 2
WIDE = HEADS * HD
VMEM = 8 * 1024 * 1024
BF = jnp.bfloat16
F32 = jnp.float32


def dot(left, right):
    return jnp.dot(left, right, preferred_element_type=F32)


def dot_nt(left, right):
    return lax.dot_general(left, right, (((1,), (1,)), ((), ())), preferred_element_type=F32)


def dot_tn(left, right):
    return lax.dot_general(left, right, (((0,), (0,)), ((), ())), preferred_element_type=F32)


def phi(before):
    return jnp.where(before > 0, before + 1.0, jnp.exp(jnp.minimum(before, 0.0)))


def col(head):
    return slice(head * HD, (head + 1) * HD)


def col_of(half, head):
    return pl.ds(pl.multiple_of(half * (HALF * HD) + head * HD, HD), HD)


def own_half():
    return lax.axis_index("seq") % 2


def lin_scale(tokens):
    return 1.0 / (HD * tokens * lax.axis_size("seq"))


def cost(microseconds):
    return pl.CostEstimate(
        flops=int(microseconds * 1000), bytes_accessed=1000, transcendentals=0
    )


def array(shape, kind):
    return jax.ShapeDtypeStruct(shape, kind)


def call(kernel, name, outs, operands, in_hbm=0, unread=0, microseconds=3, **more):
    whole = pl.BlockSpec(memory_space=pltpu.VMEM)
    return pl.pallas_call(
        kernel,
        in_specs=[pl.BlockSpec(memory_space=pltpu.HBM)] * in_hbm
        + [whole] * (len(operands) - in_hbm - unread)
        + [pl.BlockSpec(memory_space=pl.ANY)] * unread,
        out_specs=[whole] * len(outs),
        out_shape=outs,
        cost_estimate=cost(microseconds),
        compiler_params=pltpu.CompilerParams(vmem_limit_bytes=VMEM),
        name=name,
        **more,
    )(*operands)


def feature_kernel(first, lq, lk, v, g, fm, *rest):
    fq_out, fk_out, *t_out, rows, maps, arrived = rest[-5 - CHUNKS :]
    half = 1 - own_half() if first else own_half()

    def copies(step):
        head = half * HALF + step * GROUP
        wide = pl.ds(pl.multiple_of(head * HD, GROUP * HD), GROUP * HD)
        here = slice(step * GROUP * HD, (step + 1) * GROUP * HD)
        pairs = [(ref.at[:, wide], rows.at[n, :, here]) for n, ref in enumerate((lq, lk, v, g))]
        pairs.append((fm.at[pl.ds(head, GROUP)], maps.at[step * GROUP : (step + 1) * GROUP]))
        return [
            pltpu.make_async_copy(source, target, arrived.at[step, n])
            for n, (source, target) in enumerate(pairs)
        ]

    started = [copies(step) for step in range(HALF // GROUP)]
    for step in started:
        for copy in step:
            copy.start()
    for h in range(HALF):
        if h % GROUP == 0:
            for copy in started[h // GROUP]:
                copy.wait()
        c = col(h)
        w = maps[h]
        fq = phi(dot(rows[0, :, c], w)).astype(BF)
        fk = phi(dot(rows[1, :, c], w)).astype(BF)
        fq_out[:, c] = fq
        fk_out[:, c] = fk
        t_out[h // CHUNK][0, h % CHUNK] = dot_tn(fk, rows[2, :, c]).astype(BF)
        t_out[h // CHUNK][1, h % CHUNK] = dot_tn(fq, rows[3, :, c]).astype(BF)


def features(lq, lk, v, g, fm, follows):
    tokens = lq.shape[0]
    row = array((tokens, HALF * HD), BF)
    lq, lk, v, g, fm = (pltpu.with_memory_space_constraint(x, pltpu.HBM) for x in (lq, lk, v, g, fm))
    return call(
        functools.partial(feature_kernel, not follows),
        "features",
        [row, row] + [array((2, CHUNK, HD, HD), BF)] * CHUNKS,
        (lq, lk, v, g, fm, *follows),
        in_hbm=5,
        unread=len(follows),
        scratch_shapes=[
            pltpu.VMEM((4, tokens, HALF * HD), BF),
            pltpu.VMEM((HALF, HD, HD), BF),
            pltpu.SemaphoreType.DMA((HALF // GROUP, 5)),
        ],
    )


def causal_mask(tokens):
    rows = lax.broadcasted_iota(jnp.int32, (tokens, tokens), 0)
    cols = lax.broadcasted_iota(jnp.int32, (tokens, tokens), 1)
    return rows >= cols


def window_kernel(wq, wk, v, g, rims, *rest):
    att, dv, dwq, dwk, tail_k, send = rest[-6:]
    tokens = wq.shape[0]
    root = HD ** (-0.5)
    rows = lax.broadcasted_iota(jnp.int32, (tokens, 2 * WINDOW), 0)
    cols = lax.broadcasted_iota(jnp.int32, (tokens, 2 * WINDOW), 1)
    offset = cols - rows % WINDOW
    absent = (lax.axis_index("seq") == 0) & (rows < WINDOW) & (cols < WINDOW)
    band = (offset >= 1) & (offset <= WINDOW) & jnp.logical_not(absent)
    for h in range(HEADS):
        c = col(h)
        q, k, val, grad = wq[:, c], wk[:, c], v[:, c], g[:, c]
        kp = jnp.concatenate([rims[0, :, c], k[:WINDOW]], axis=0)
        vp = jnp.concatenate([rims[1, :, c], val[:WINDOW]], axis=0)
        score = jnp.concatenate([dot_nt(q[:WINDOW], kp), dot_nt(q[WINDOW:], k)], axis=0) * root
        score = jnp.where(band, score, -jnp.inf)
        expo = jnp.exp(score - jnp.max(score, axis=-1, keepdims=True))
        prob = expo / jnp.sum(expo, axis=-1, keepdims=True)
        prob_b = prob.astype(BF)
        dprob = jnp.concatenate([dot_nt(grad[:WINDOW], vp), dot_nt(grad[WINDOW:], val)], axis=0)
        delta = jnp.sum(prob * dprob, axis=-1, keepdims=True)
        dscore = (prob * (dprob - delta) * root).astype(BF)
        win = jnp.concatenate([dot(prob_b[:WINDOW], vp), dot(prob_b[WINDOW:], val)], axis=0)
        att[:, c] = win
        dwq[:, c] = jnp.concatenate(
            [dot(dscore[:WINDOW], kp), dot(dscore[WINDOW:], k)], axis=0
        ).astype(BF)
        dk0 = dot_tn(dscore[:WINDOW], q[:WINDOW])
        dk1 = dot_tn(dscore[WINDOW:], q[WINDOW:])
        dv0 = dot_tn(prob_b[:WINDOW], grad[:WINDOW])
        dv1 = dot_tn(prob_b[WINDOW:], grad[WINDOW:])
        send[0, :, c] = dk0[:WINDOW].astype(BF)
        send[1, :, c] = dv0[:WINDOW].astype(BF)
        dwk[:, c] = jnp.concatenate([dk0[WINDOW:] + dk1[:WINDOW], dk1[WINDOW:]], axis=0).astype(BF)
        tail_k[:, c] = dk1[WINDOW:]
        dv[:, c] = jnp.concatenate([dv0[WINDOW:] + dv1[:WINDOW], dv1[WINDOW:]], axis=0)


def window_part(*operands):
    tokens = operands[0].shape[0]
    wide, narrow = array((tokens, WIDE), F32), array((tokens, WIDE), BF)
    return call(
        window_kernel,
        "window_part",
        [wide, wide, narrow, narrow, array((WINDOW, WIDE), F32), array((2, WINDOW, WIDE), BF)],
        operands,
        unread=len(operands) - 5,
        microseconds=6,
    )


def state_kernel(first, count, lq, lk, v, g, fq, fk, *rest):
    states, (dpq_out, dpk_out, keep, send) = rest[:count], rest[-4:]
    core, far = lax.axis_index("dp") % 2, lax.axis_index("dp") // 2
    half = own_half() if count == CHUNKS else 1 - own_half()
    scale = lin_scale(lq.shape[0])
    causal = causal_mask(lq.shape[0])
    if 0 < first:
        keep[:, :first] = rest[count][...]
        send[:, :first] = rest[count + 1][...]
    for n in range(count):
        terms = []
        for h in range(CHUNK):
            head = (first + n) * CHUNK + h
            c, at, here = col(head), col_of(half, head), col(n * CHUNK + h)
            q_feat, k_feat, val, grad = fq[:, c], fk[:, c], v[:, at], g[:, at]
            mixed = jnp.where(causal, dot_nt(grad, val), 0.0).astype(BF)
            dfq = (dot(mixed, k_feat) + dot_nt(grad, states[n][0, h])) * scale
            dfk = (dot_tn(mixed, q_feat) + dot_nt(val, states[n][1, h])) * scale
            dpq = (dfq * jnp.minimum(q_feat.astype(F32), 1.0)).astype(BF)
            dpk = (dfk * jnp.minimum(k_feat.astype(F32), 1.0)).astype(BF)
            dpq_out[:, here], dpk_out[:, here] = dpq, dpk
            terms.append((dot_tn(lq[:, at], dpq) + dot_tn(lk[:, at], dpk)).astype(BF))
        for y in range(2):
            keep[y ^ far, first + n] = jnp.where(core == 0, terms[y], terms[2 + y])
            send[y ^ far, first + n] = jnp.where(core == 0, terms[2 + y], terms[y])


def state_part(first, count, arrays, states, earlier, follows=()):
    row = array((arrays[0].shape[0], count * CHUNK * HD), BF)
    part = array((2, first + count, HD, HD), BF)
    return call(
        functools.partial(state_kernel, first, count),
        "state_part",
        [row, row, part, part],
        (*arrays, *states, *earlier, *follows),
        unread=len(follows),
    )


def output_kernel(v, g, fm, win, dv_win, *rest):
    att, dlq, dlk, dv, tail_v = rest[-5:]
    scale = lin_scale(win.shape[0])
    own = own_half()
    causal = causal_mask(v.shape[0])
    for half, refs in ((own, rest[: 4 + CHUNKS]), (1 - own, rest[4 + CHUNKS : -5])):
        fq, fk = refs[:2]
        states, pairs = refs[2 : 2 + CHUNKS], refs[2 + CHUNKS :]
        for h in range(HALF):
            n, k = h // CHUNK, h % CHUNK
            c, at = col(h), col_of(half, h)
            w = fm[half * HALF + h]
            each = 2 * HALF // len(pairs)
            m, here = 2 * (h // each), col(h % each)
            dlq[:, at] = dot_nt(pairs[m][:, here], w).astype(BF)
            dlk[:, at] = dot_nt(pairs[m + 1][:, here], w).astype(BF)
            q_feat, k_feat = fq[:, c], fk[:, c]
            scores = jnp.where(causal, dot_nt(q_feat, k_feat), 0.0).astype(BF)
            lin = dot(scores, v[:, at]) + dot(q_feat, states[n][0, k])
            att[:, at] = (lin * scale + win[:, at]).astype(BF)
            grad_v = dot_tn(scores, g[:, at]) + dot(k_feat, states[n][1, k])
            grad_v = grad_v * scale + dv_win[:, at]
            dv[:, at] = grad_v.astype(BF)
            tail_v[:, at] = grad_v[WINDOW:]


def output_part(v, g, fm, win, dv_win, own, other):
    row = array(win.shape, BF)
    return call(
        output_kernel,
        "output_part",
        [row] * 4 + [array((WINDOW, WIDE), F32)],
        (v, g, fm, win, dv_win, *own, *other),
    )


def finish_kernel(tail_k, tail_v, rims, k_in, v_in, dk, dv):
    dk[...] = (tail_k[...] + rims[0].astype(F32)).astype(BF)
    dv[...] = (tail_v[...] + rims[1].astype(F32)).astype(BF)


def finish(tail_k, tail_v, back, dwk, dv):
    rims = pl.BlockSpec((WINDOW, WIDE), lambda i: (0, 0))
    last = pl.BlockSpec((WINDOW, WIDE), lambda i: (dwk.shape[0] // WINDOW - 1, 0))
    kept = pl.BlockSpec(memory_space=pl.ANY)
    row = jax.ShapeDtypeStruct(dwk.shape, BF)
    return pl.pallas_call(
        finish_kernel,
        grid=(1,),
        in_specs=[rims] * 2 + [pl.BlockSpec(back.shape, lambda i: (0, 0, 0))] + [kept] * 2,
        out_specs=[last, last],
        out_shape=[row, row],
        input_output_aliases={3: 0, 4: 1},
        cost_estimate=cost(1),
        compiler_params=pltpu.CompilerParams(vmem_limit_bytes=VMEM),
        name="finish",
    )(tail_k, tail_v, back, dwk, dv)


def flipped(block, bit):
    count = lax.axis_size("seq")
    return lax.ppermute(block, "seq", [(i, i ^ bit) for i in range(count)])


def flat_flipped(block, seq_bits, dp_bits):
    rows, width = lax.axis_size("seq"), lax.axis_size("dp")
    route = [
        (s * width + d, (s ^ seq_bits) * width + (d ^ dp_bits))
        for s in range(rows)
        for d in range(width)
    ]
    return lax.ppermute(block, ("seq", "dp"), route)


def passed_along(block, distance):
    devices = range(lax.axis_size("seq"))
    route = [(i - distance, i) for i in devices if i - distance in devices]
    return lax.ppermute(block, "seq", route)


def spread(block, level):
    count = lax.axis_size("seq")
    size = 2 << level
    total = None
    for turn in range(1 << level):
        route = []
        for base in range(0, count // 2, size):
            low, high = base + size // 2 - 1, base + size // 2
            for parity in range(2):
                route.append((2 * low + parity, 2 * (high + turn) + parity))
                route.append((2 * high + parity, 2 * (low - turn) + parity))
        came = lax.ppermute(block, "seq", route)
        total = came if total is None else total + came
    return total


def levels():
    return (lax.axis_size("seq") // 2).bit_length() - 1


def upper(level):
    return ((lax.axis_index("seq") // 2) >> level) % 2 == 1


def outgoing(pair, sums, level):
    total = pair if sums is None else pair.astype(F32) + sums.astype(F32)
    return jnp.where(upper(level), total[1], total[0]).astype(BF)


def taken(sums, got, level):
    side = lax.broadcasted_iota(jnp.int32, (2, 1, 1, 1), 0)
    here = jnp.where((side == 0) == upper(level), got[None], jnp.zeros_like(got)[None])
    return here if sums is None else (sums.astype(F32) + here.astype(F32)).astype(BF)


def entering(sums, kept, came):
    side = lax.broadcasted_iota(jnp.int32, (2, 1, 1, 1), 0)
    same = side == own_half()
    added = (jnp.where(same, jnp.zeros_like(came), came), jnp.where(same, kept, jnp.zeros_like(kept)))
    return [(sums.astype(F32) + x.astype(F32)).astype(BF) for x in added]


def near_sum(keep, send):
    return (keep.astype(F32) + flat_flipped(send, 0, 1).astype(F32)).astype(BF)


def assemble_kernel(norm, *refs):
    pieces, out = refs[:-1], refs[-1]
    core, far = lax.axis_index("dp") % 2, lax.axis_index("dp") // 2
    for side in range(2):
        half = own_half() ^ side
        for n in range(CHUNKS):
            for c in range(2):
                for y in range(2):
                    head = half * HALF + n * CHUNK + (c ^ core) * 2 + (y ^ far)
                    out[head] = pieces[side * 4 + c * 2 + y][n].astype(F32) * norm


def assemble(pieces, norm):
    return call(
        functools.partial(assemble_kernel, norm), "assemble", [array((HEADS, HD, HD), F32)], pieces
    )[0]


def on_device(
    linear_queries, linear_keys, window_queries, window_keys, values, cotangent, feature_map
):
    tokens = linear_queries.shape[1]
    total_tokens = tokens * lax.axis_size("seq") * lax.axis_size("dp") * linear_queries.shape[0]
    lq, lk, wq, wk, v, g = (
        x[0]
        for x in (linear_queries, linear_keys, window_queries, window_keys, values, cotangent)
    )
    fq_o, fk_o, *given = features(lq, lk, v, g, feature_map, ())
    came = [flipped(x, 1) for x in given]
    fq, fk, *kept = features(lq, lk, v, g, feature_map, (fq_o,))
    pair = [(a.astype(F32) + b.astype(F32)).astype(BF) for a, b in zip(kept, came)]
    sums = [None] * CHUNKS
    for level in range(levels()):
        sent = [outgoing(pair[n], sums[n], level) for n in range(CHUNKS)]
        if level == 0:
            tails = jnp.stack([wk[tokens - WINDOW :], v[tokens - WINDOW :]])
            sent[0], tails = lax.optimization_barrier((sent[0], tails))
            rims = passed_along(tails, 1)
        for n in range(CHUNKS):
            got = spread(sent[n], level)
            if level == levels() - 1 and n == CHUNKS - 1:
                got, rims = lax.optimization_barrier((got, rims))
            sums[n] = taken(sums[n], got, level)
    mine, others = zip(*(entering(sums[n], kept[n], came[n]) for n in range(CHUNKS)))
    rows = (lq, lk, v, g)
    back = [flipped(x, 1) for x in others]
    win, dv_win, dwq, dwk, tail_k, edge = window_part(wq, wk, v, g, rims, others[-1])
    dpq, dpk, *near = state_part(0, CHUNKS, (*rows, fq, fk), mine, (), (dwq,))
    own = (fq, fk, *mine, dpq, dpk)
    beyond, pairs = (), []
    for n in range(CHUNKS):
        dpq, dpk, *beyond = state_part(n, 1, (*rows, fq_o, fk_o), (back[n],), beyond, (dwq,))
        pairs += [dpq, dpk]
    other = (fq_o, fk_o, *back, *pairs)
    near, beyond = lax.optimization_barrier((near, beyond))
    near, beyond = near_sum(*near), near_sum(*beyond)
    a, c = flat_flipped(beyond[0], 1, 0), flat_flipped(beyond[1], 1, 2)
    b = flat_flipped(near[1], 0, 2)
    total = sum(x.astype(F32) for x in (near[0], a, b, c))
    sent, edge = lax.optimization_barrier((total.astype(BF), edge))
    total = sent.astype(F32)
    for bits in range(2, lax.axis_size("seq"), 2):
        total = total + flat_flipped(sent, bits, 0).astype(F32)
    edge = passed_along(edge, -1)
    done = total.astype(BF)
    a, b, c = flat_flipped(done, 1, 0), flat_flipped(done, 0, 2), flat_flipped(done, 1, 2)
    across = [flat_flipped(x, 0, 1) for x in (done, b, a, c)]
    map_grad = assemble(
        (done, b, *across[:2], a, c, *across[2:]), total_tokens ** (-0.5)
    )
    attended, dlq, dlk, dv, tail_v = output_part(v, g, feature_map, win, dv_win, own, other)
    dwk, dv = finish(tail_k, tail_v, edge, dwk, dv)
    return attended[None], dlq[None], dlk[None], dwq[None], dwk[None], dv[None], map_grad


def solution(mesh):
    row = P("dp", "seq", None)
    return jax.shard_map(
        on_device,
        mesh=mesh,
        in_specs=(row,) * 6 + (P(),),
        out_specs=(row,) * 6 + (P(),),
        check_vma=False,
    )
```

```python
import functools

import jax
import jax.numpy as jnp
from jax import lax
from jax.experimental import pallas as pl
from jax.experimental.pallas import tpu as pltpu
from jax.sharding import PartitionSpec as P

HEADS = 16
HD = 128
WINDOW = 64
HALF = HEADS // 2
CHUNKS = 2
CHUNK = HALF // CHUNKS
GROUP = 2
WINDOW_GROUP = 4
WIDE = HEADS * HD
VMEM = 8 * 1024 * 1024
BF = jnp.bfloat16
F32 = jnp.float32


def dot(left, right):
    return jnp.dot(left, right, preferred_element_type=F32)


def dot_nt(left, right):
    return lax.dot_general(left, right, (((1,), (1,)), ((), ())), preferred_element_type=F32)


def dot_tn(left, right):
    return lax.dot_general(left, right, (((0,), (0,)), ((), ())), preferred_element_type=F32)


def phi(before):
    return jnp.where(before > 0, before + 1.0, jnp.exp(jnp.minimum(before, 0.0)))


def col(head):
    return slice(head * HD, (head + 1) * HD)


def col_of(half, head):
    return pl.ds(pl.multiple_of(half * (HALF * HD) + head * HD, HD), HD)


def own_half():
    return lax.axis_index("seq") % 2


def lin_scale(tokens):
    return 1.0 / (HD * tokens * lax.axis_size("seq"))


def cost(microseconds):
    return pl.CostEstimate(
        flops=int(microseconds * 1000), bytes_accessed=1000, transcendentals=0
    )


def array(shape, kind):
    return jax.ShapeDtypeStruct(shape, kind)


def call(kernel, name, outs, operands, in_hbm=0, unread=0, microseconds=3, **more):
    whole = pl.BlockSpec(memory_space=pltpu.VMEM)
    return pl.pallas_call(
        kernel,
        in_specs=[pl.BlockSpec(memory_space=pltpu.HBM)] * in_hbm
        + [whole] * (len(operands) - in_hbm - unread)
        + [pl.BlockSpec(memory_space=pl.ANY)] * unread,
        out_specs=[whole] * len(outs),
        out_shape=outs,
        cost_estimate=cost(microseconds),
        compiler_params=pltpu.CompilerParams(vmem_limit_bytes=VMEM),
        name=name,
        **more,
    )(*operands)


def feature_kernel(first, lq, lk, v, g, fm, *rest):
    fq_out, fk_out, *t_out, rows, maps, arrived = rest[-5 - CHUNKS :]
    half = 1 - own_half() if first else own_half()

    def copies(step):
        head = half * HALF + step * GROUP
        wide = pl.ds(pl.multiple_of(head * HD, GROUP * HD), GROUP * HD)
        here = slice(step * GROUP * HD, (step + 1) * GROUP * HD)
        pairs = [(ref.at[:, wide], rows.at[n, :, here]) for n, ref in enumerate((lq, lk, v, g))]
        pairs.append((fm.at[pl.ds(head, GROUP)], maps.at[step * GROUP : (step + 1) * GROUP]))
        return [
            pltpu.make_async_copy(source, target, arrived.at[step, n])
            for n, (source, target) in enumerate(pairs)
        ]

    started = [copies(step) for step in range(HALF // GROUP)]
    for step in started:
        for copy in step:
            copy.start()
    for step, arriving in enumerate(started):
        for copy in arriving:
            copy.wait()
        heads = range(step * GROUP, (step + 1) * GROUP)
        pre = [(dot(rows[0, :, col(h)], maps[h]), dot(rows[1, :, col(h)], maps[h])) for h in heads]
        feats = [(phi(q).astype(BF), phi(k).astype(BF)) for q, k in pre]
        for h, (fq, fk) in zip(heads, feats):
            fq_out[:, col(h)], fk_out[:, col(h)] = fq, fk
        sums = [
            (dot_tn(fk, rows[2, :, col(h)]), dot_tn(fq, rows[3, :, col(h)]))
            for h, (fq, fk) in zip(heads, feats)
        ]
        for h, (forward, backward) in zip(heads, sums):
            t_out[h // CHUNK][0, h % CHUNK] = forward.astype(BF)
            t_out[h // CHUNK][1, h % CHUNK] = backward.astype(BF)


def features(lq, lk, v, g, fm, follows):
    tokens = lq.shape[0]
    row = array((tokens, HALF * HD), BF)
    lq, lk, v, g, fm = (pltpu.with_memory_space_constraint(x, pltpu.HBM) for x in (lq, lk, v, g, fm))
    return call(
        functools.partial(feature_kernel, not follows),
        "features",
        [row, row] + [array((2, CHUNK, HD, HD), BF)] * CHUNKS,
        (lq, lk, v, g, fm, *follows),
        in_hbm=5,
        unread=len(follows),
        scratch_shapes=[
            pltpu.VMEM((4, tokens, HALF * HD), BF),
            pltpu.VMEM((HALF, HD, HD), BF),
            pltpu.SemaphoreType.DMA((HALF // GROUP, 5)),
        ],
    )


def causal_mask(tokens):
    rows = lax.broadcasted_iota(jnp.int32, (tokens, tokens), 0)
    cols = lax.broadcasted_iota(jnp.int32, (tokens, tokens), 1)
    return rows >= cols


def window_kernel(wq, wk, v, g, rims, *rest):
    win, dv, dwq, dwk, edge = rest[-5:]
    tokens = wq.shape[0]
    root = HD ** (-0.5)
    rows = lax.broadcasted_iota(jnp.int32, (tokens, 2 * WINDOW), 0)
    cols = lax.broadcasted_iota(jnp.int32, (tokens, 2 * WINDOW), 1)
    offset = cols - rows % WINDOW
    absent = (lax.axis_index("seq") == 0) & (rows < WINDOW) & (cols < WINDOW)
    band = (offset >= 1) & (offset <= WINDOW) & jnp.logical_not(absent)
    blocks = range(tokens // WINDOW)

    def rows_of(block):
        return slice(block * WINDOW, (block + 1) * WINDOW)

    def pairs(ref, rim, c):
        first = jnp.concatenate([rims[rim, :, c], ref[:WINDOW, c]], axis=0)
        return [first] + [ref[(n - 1) * WINDOW : (n + 1) * WINDOW, c] for n in blocks[1:]]

    def by_block(form, lefts, rights):
        return jnp.concatenate([form(a, b) for a, b in zip(lefts, rights)], axis=0)

    for start in range(0, HEADS, WINDOW_GROUP):
        at = [col(h) for h in range(start, start + WINDOW_GROUP)]
        q = [[wq[rows_of(n), c] for n in blocks] for c in at]
        grad = [[g[rows_of(n), c] for n in blocks] for c in at]
        keys, vals = [pairs(wk, 0, c) for c in at], [pairs(v, 1, c) for c in at]
        score = [by_block(dot_nt, a, b) for a, b in zip(q, keys)]
        dprob = [by_block(dot_nt, a, b) for a, b in zip(grad, vals)]
        score = [jnp.where(band, x * root, -jnp.inf) for x in score]
        top = [jnp.max(x, axis=-1, keepdims=True) for x in score]
        expo = [jnp.exp(x - y) for x, y in zip(score, top)]
        prob = [x / jnp.sum(x, axis=-1, keepdims=True) for x in expo]
        delta = [jnp.sum(x * y, axis=-1, keepdims=True) for x, y in zip(prob, dprob)]
        dscore = [
            (x * (y - z) * root).astype(BF) for x, y, z in zip(prob, dprob, delta)
        ]
        prob = [x.astype(BF) for x in prob]
        prob = [[x[rows_of(n)] for n in blocks] for x in prob]
        dscore = [[x[rows_of(n)] for n in blocks] for x in dscore]
        for i, c in enumerate(at):
            win[:, c] = by_block(dot, prob[i], vals[i])
            dwq[:, c] = by_block(dot, dscore[i], keys[i]).astype(BF)
        for i, c in enumerate(at):
            dk = [dot_tn(x, y) for x, y in zip(dscore[i], q[i])]
            dval = [dot_tn(x, y) for x, y in zip(prob[i], grad[i])]
            edge[0, :, c], edge[1, :, c] = dk[0][:WINDOW].astype(BF), dval[0][:WINDOW].astype(BF)
            for n in blocks:
                more = n + 1 < len(blocks)
                a, b = dk[n][WINDOW:], dval[n][WINDOW:]
                dwk[rows_of(n), c] = a + dk[n + 1][:WINDOW] if more else a
                dv[rows_of(n), c] = b + dval[n + 1][:WINDOW] if more else b


def window_part(*operands):
    wide = array(operands[0].shape, F32)
    return call(
        window_kernel,
        "window_part",
        [wide, wide, array(wide.shape, BF), wide, array((2, WINDOW, WIDE), BF)],
        operands,
        unread=len(operands) - 5,
    )


def state_kernel(first, count, lq, lk, v, g, fq, fk, *rest):
    states, (dpq_out, dpk_out, keep, send) = rest[:count], rest[-4:]
    core, far = lax.axis_index("dp") % 2, lax.axis_index("dp") // 2
    side = 0 if count == CHUNKS else 1
    half = own_half() if side == 0 else 1 - own_half()
    scale = lin_scale(lq.shape[0])
    causal = causal_mask(lq.shape[0])
    if side == 1:
        keep[0], send[0] = rest[count][0], rest[count + 1][0]
        if first > 0:
            keep[1, :, :first] = rest[count][1, :, :first]
            send[1, :, :first] = rest[count + 1][1, :, :first]
    for n in range(count):
        heads = [(first + n) * CHUNK + h for h in range(CHUNK)]
        at = [col_of(half, head) for head in heads]
        q_feat, k_feat = [fq[:, col(x)] for x in heads], [fk[:, col(x)] for x in heads]
        val, grad = [v[:, x] for x in at], [g[:, x] for x in at]
        mixed = [jnp.where(causal, dot_nt(a, b), 0.0).astype(BF) for a, b in zip(grad, val)]
        dfq = [dot_nt(a, states[n][0, h]) for h, a in enumerate(grad)]
        dfk = [dot_nt(a, states[n][1, h]) for h, a in enumerate(val)]
        dfq = [(a + dot(b, c)) * scale for a, b, c in zip(dfq, mixed, k_feat)]
        dfk = [(a + dot_tn(b, c)) * scale for a, b, c in zip(dfk, mixed, q_feat)]
        dpq = [(a * jnp.minimum(b.astype(F32), 1.0)).astype(BF) for a, b in zip(dfq, q_feat)]
        dpk = [(a * jnp.minimum(b.astype(F32), 1.0)).astype(BF) for a, b in zip(dfk, k_feat)]
        terms = [
            (dot_tn(lq[:, x], a) + dot_tn(lk[:, x], b)).astype(BF)
            for x, a, b in zip(at, dpq, dpk)
        ]
        for h in range(CHUNK):
            here = col(n * CHUNK + h)
            dpq_out[:, here], dpk_out[:, here] = dpq[h], dpk[h]
        for y in range(2):
            keep[side, y ^ far, first + n] = jnp.where(core == 0, terms[y], terms[2 + y])
            send[side, y ^ far, first + n] = jnp.where(core == 0, terms[2 + y], terms[y])


def state_part(first, count, arrays, states, earlier, follows=()):
    row = array((arrays[0].shape[0], count * CHUNK * HD), BF)
    part = array((2, 2, CHUNKS, HD, HD), BF)
    return call(
        functools.partial(state_kernel, first, count),
        "state_part",
        [row, row, part, part],
        (*arrays, *states, *earlier, *follows),
        unread=len(follows),
    )


def output_kernel(v, g, fm, win, dv_win, dq, dk, edge, *rest):
    att, dlq, dlk, dv, dwq, dwk, token = rest[-7:]
    token[...] = jnp.zeros_like(token)
    scale = lin_scale(v.shape[0])
    causal = causal_mask(v.shape[0])
    tail = v.shape[0] - WINDOW
    dwq[...] = dq[...]
    dwk[:tail] = dk[:tail].astype(BF)
    dwk[tail:] = (dk[tail:] + edge[0].astype(F32)).astype(BF)
    for side in range(2):
        half = own_half() ^ side
        refs = rest[: 2 + CHUNKS + 2] if side == 0 else rest[2 + CHUNKS + 2 : -7]
        fq, fk = refs[:2]
        states, pairs = refs[2 : 2 + CHUNKS], refs[2 + CHUNKS :]
        each = 2 * HALF // len(pairs)
        for n in range(CHUNKS):
            heads = [n * CHUNK + k for k in range(CHUNK)]
            cols = [(col(h), col_of(half, h)) for h in heads]
            scores = [
                jnp.where(causal, dot_nt(fq[:, c], fk[:, c]), 0.0).astype(BF) for c, _ in cols
            ]
            for h, (_, at) in zip(heads, cols):
                m, here, w = 2 * (h // each), col(h % each), fm[half * HALF + h]
                dlq[:, at] = dot_nt(pairs[m][:, here], w).astype(BF)
                dlk[:, at] = dot_nt(pairs[m + 1][:, here], w).astype(BF)
            lin = [dot(fq[:, c], states[n][0, k]) for k, (c, _) in enumerate(cols)]
            grad_v = [dot(fk[:, c], states[n][1, k]) for k, (c, _) in enumerate(cols)]
            for k, (_, at) in enumerate(cols):
                out = (lin[k] + dot(scores[k], v[:, at])) * scale
                att[:, at] = (out + win[:, at]).astype(BF)
                out = (grad_v[k] + dot_tn(scores[k], g[:, at])) * scale + dv_win[:, at]
                dv[:tail, at] = out[:tail].astype(BF)
                dv[tail:, at] = (out[tail:] + edge[1, :, at].astype(F32)).astype(BF)


def output_part(v, g, fm, windows, own, other):
    row = array(v.shape, BF)
    return call(
        output_kernel, "output_part", [row] * 6 + [array((8, HD), F32)], (v, g, fm, *windows, *own, *other)
    )


def flipped(block, bit):
    count = lax.axis_size("seq")
    return lax.ppermute(block, "seq", [(i, i ^ bit) for i in range(count)])


def flat_flipped(block, seq_bits, dp_bits):
    rows, width = lax.axis_size("seq"), lax.axis_size("dp")
    route = [
        (s * width + d, (s ^ seq_bits) * width + (d ^ dp_bits))
        for s in range(rows)
        for d in range(width)
    ]
    return lax.ppermute(block, ("seq", "dp"), route)


def passed_along(block, distance):
    devices = range(lax.axis_size("seq"))
    route = [(i - distance, i) for i in devices if i - distance in devices]
    return lax.ppermute(block, "seq", route)


def spread(block, level):
    count = lax.axis_size("seq")
    size = 2 << level
    arrived = []
    for turn in range(1 << level):
        route = []
        for base in range(0, count // 2, size):
            low, high = base + size // 2 - 1, base + size // 2
            for parity in range(2):
                route.append((2 * low + parity, 2 * (high + turn) + parity))
                route.append((2 * high + parity, 2 * (low - turn) + parity))
        arrived.append(lax.ppermute(block, "seq", route))
    return arrived


def levels():
    return (lax.axis_size("seq") // 2).bit_length() - 1


def upper(level):
    return ((lax.axis_index("seq") // 2) >> level) % 2 == 1


def sides(gots):
    low = high = None
    for level, arrived in enumerate(gots):
        got = sum(x[...].astype(F32) for x in arrived)
        above = upper(level)
        a, b = jnp.where(above, got, 0.0), jnp.where(above, 0.0, got)
        low, high = (a, b) if low is None else (low + a, high + b)
    return low, high


def by_level(refs):
    gots, at = [], 0
    while at < len(refs):
        count = 1 << len(gots)
        gots.append(refs[at : at + count])
        at += count
    return gots


def pair_kernel(kept, came, pair, send):
    total = kept[...].astype(F32) + came[...].astype(F32)
    pair[...] = total.astype(BF)
    send[...] = jnp.where(upper(0), total[1], total[0]).astype(BF)


def pair_sum(kept, came):
    return call(
        pair_kernel, "pair_sum", [array(kept.shape, BF), array(kept.shape[1:], BF)], (kept, came)
    )


def level_kernel(pair, *refs):
    *gots, send = refs
    gots = by_level(gots)
    low, high = sides(gots)
    above = upper(len(gots))
    send[...] = jnp.where(
        above, pair[1].astype(F32) + high, pair[0].astype(F32) + low
    ).astype(BF)


def level_sum(pair, gots):
    return call(level_kernel, "level_sum", [array(pair.shape[1:], BF)], (pair, *gots))[0]


def entering_kernel(kept, came, *refs):
    *gots, mine, others = refs
    low, high = sides(by_level(gots))
    zero = jnp.zeros_like(low)
    low, high = (zero, zero) if low is None else (low, high)
    first = own_half() == 0
    mine[0] = (low + jnp.where(first, zero, came[0].astype(F32))).astype(BF)
    mine[1] = (high + jnp.where(first, came[1].astype(F32), zero)).astype(BF)
    others[0] = (low + jnp.where(first, kept[0].astype(F32), zero)).astype(BF)
    others[1] = (high + jnp.where(first, zero, kept[1].astype(F32))).astype(BF)


def entering(kept, came, gots):
    return call(
        entering_kernel, "entering", [array(kept.shape, BF)] * 2, (kept, came, *gots)
    )


def near_kernel(keep, came, mine, a, b, c):
    def total(side, y):
        return keep[side, y].astype(F32) + came[side, y].astype(F32)

    mine[...] = total(0, 0)
    a[...], b[...], c[...] = (total(*at).astype(BF) for at in ((1, 0), (0, 1), (1, 1)))


def near_sum(keep, came):
    part = array(keep.shape[2:], BF)
    return call(
        near_kernel, "near_sum", [array(part.shape, F32), part, part, part], (keep, came)
    )


def total_kernel(count, *refs):
    refs[-1][...] = sum(x[...].astype(F32) for x in refs[:count]).astype(BF)


def total_of(arrays, follows=()):
    return call(
        functools.partial(total_kernel, len(arrays)),
        "total",
        [array(arrays[0].shape, BF)],
        (*arrays, *follows),
        unread=len(follows),
    )[0]


def assemble_kernel(norm, *refs):
    pieces, out = refs[:-1], refs[-1]
    core, far = lax.axis_index("dp") % 2, lax.axis_index("dp") // 2
    for side in range(2):
        half = own_half() ^ side
        for n in range(CHUNKS):
            for c in range(2):
                for y in range(2):
                    head = half * HALF + n * CHUNK + (c ^ core) * 2 + (y ^ far)
                    out[head] = pieces[side * 4 + c * 2 + y][n].astype(F32) * norm


def assemble(pieces, norm):
    return call(
        functools.partial(assemble_kernel, norm), "assemble", [array((HEADS, HD, HD), F32)], pieces
    )[0]


def on_device(
    linear_queries, linear_keys, window_queries, window_keys, values, cotangent, feature_map
):
    tokens = linear_queries.shape[1]
    total_tokens = tokens * lax.axis_size("seq") * lax.axis_size("dp") * linear_queries.shape[0]
    lq, lk, wq, wk, v, g = (
        x[0]
        for x in (linear_queries, linear_keys, window_queries, window_keys, values, cotangent)
    )
    fq_o, fk_o, *given = features(lq, lk, v, g, feature_map, ())
    came = [flipped(x, 1) for x in given]
    ends = jnp.stack([wk[tokens - WINDOW :], v[tokens - WINDOW :]])
    fq, fk, *kept = features(lq, lk, v, g, feature_map, (fq_o,))
    pair, sent = zip(*(pair_sum(a, b) for a, b in zip(kept, came)))
    pair, sent = list(pair), list(sent)
    gots = [[] for _ in range(CHUNKS)]
    for level in range(levels()):
        if level > 0:
            sent = [level_sum(pair[n], gots[n]) for n in range(CHUNKS)]
        for n in range(CHUNKS):
            gots[n] += spread(sent[n], level)
            if level == 0 and n == CHUNKS - 1:
                gots[n], ends = lax.optimization_barrier((gots[n], ends))
                rims = passed_along(ends, 1)
    mine, others = zip(*(entering(kept[n], came[n], gots[n]) for n in range(CHUNKS)))
    back = [flipped(x, 1) for x in others]
    *windows, edge = window_part(wq, wk, v, g, rims, others[-1])
    back[-1], edge = lax.optimization_barrier((back[-1], edge))
    edge = passed_along(edge, -1)
    rows = (lq, lk, v, g)
    dpq, dpk, *terms = state_part(0, CHUNKS, (*rows, fq, fk), mine, (), (others[-1],))
    own = (fq, fk, *mine, dpq, dpk)
    pairs = []
    for n in range(CHUNKS):
        dpq, dpk, *terms = state_part(n, 1, (*rows, fq_o, fk_o), (back[n],), terms)
        pairs += [dpq, dpk]
    other = (fq_o, fk_o, *back, *pairs)
    keep, send = terms
    near, a, b, c = near_sum(keep, flat_flipped(send, 0, 1))
    a, b, c = flat_flipped(a, 1, 0), flat_flipped(b, 0, 2), flat_flipped(c, 1, 2)
    sent = total_of((near, a, b, c))
    came = [flat_flipped(sent, bits, 0) for bits in range(2, lax.axis_size("seq"), 2)]
    attended, dlq, dlk, dv, dwq, dwk, token = output_part(
        v, g, feature_map, (*windows, edge), own, other
    )
    done = total_of((sent, *came), (token,))
    a, b, c = flat_flipped(done, 1, 0), flat_flipped(done, 0, 2), flat_flipped(done, 1, 2)
    across = [flat_flipped(x, 0, 1) for x in (done, b, a, c)]
    map_grad = assemble(
        (done, b, *across[:2], a, c, *across[2:]), total_tokens ** (-0.5)
    )
    return attended[None], dlq[None], dlk[None], dwq[None], dwk[None], dv[None], map_grad


def solution(mesh):
    row = P("dp", "seq", None)
    return jax.shard_map(
        on_device,
        mesh=mesh,
        in_specs=(row,) * 6 + (P(),),
        out_specs=(row,) * 6 + (P(),),
        check_vma=False,
    )
```

```python
import functools

import jax
import jax.numpy as jnp
from jax import lax
from jax.experimental import pallas as pl
from jax.experimental.pallas import tpu as pltpu
from jax.sharding import PartitionSpec as P

HEADS = 16
HD = 128
WINDOW = 64
HALF = HEADS // 2
CHUNKS = 2
CHUNK = HALF // CHUNKS
GROUP = 2
WINDOW_GROUP = 4
WIDE = HEADS * HD
VMEM = 8 * 1024 * 1024
BF = jnp.bfloat16
F32 = jnp.float32


def dot(left, right):
    return jnp.dot(left, right, preferred_element_type=F32)


def dot_nt(left, right):
    return lax.dot_general(left, right, (((1,), (1,)), ((), ())), preferred_element_type=F32)


def dot_tn(left, right):
    return lax.dot_general(left, right, (((0,), (0,)), ((), ())), preferred_element_type=F32)


def phi(before):
    return jnp.where(before > 0, before + 1.0, jnp.exp(jnp.minimum(before, 0.0)))


def col(head):
    return slice(head * HD, (head + 1) * HD)


def col_of(half, head):
    return pl.ds(pl.multiple_of(half * (HALF * HD) + head * HD, HD), HD)


def own_half():
    return lax.axis_index("seq") % 2


def lin_scale(tokens):
    return 1.0 / (HD * tokens * lax.axis_size("seq"))


def cost(microseconds):
    return pl.CostEstimate(
        flops=int(microseconds * 1000), bytes_accessed=1000, transcendentals=0
    )


def array(shape, kind):
    return jax.ShapeDtypeStruct(shape, kind)


def call(kernel, name, outs, operands, in_hbm=0, unread=0, microseconds=3, **more):
    whole = pl.BlockSpec(memory_space=pltpu.VMEM)
    return pl.pallas_call(
        kernel,
        in_specs=[pl.BlockSpec(memory_space=pltpu.HBM)] * in_hbm
        + [whole] * (len(operands) - in_hbm - unread)
        + [pl.BlockSpec(memory_space=pl.ANY)] * unread,
        out_specs=[whole] * len(outs),
        out_shape=outs,
        cost_estimate=cost(microseconds),
        compiler_params=pltpu.CompilerParams(vmem_limit_bytes=VMEM),
        name=name,
        **more,
    )(*operands)


def feature_kernel(first, count, ends_too, lq, lk, v, g, fm, wk, *rest):
    fq_out, fk_out, *t_out, rows, maps, arrived = rest
    t_out = t_out[-count - ends_too :]
    ends = t_out.pop() if ends_too else None
    half = own_half() if count == CHUNKS else 1 - own_half()
    steps = count * CHUNK // GROUP

    def copies(step):
        head = half * HALF + first * CHUNK + step * GROUP
        wide = pl.ds(pl.multiple_of(head * HD, GROUP * HD), GROUP * HD)
        here = slice(step * GROUP * HD, (step + 1) * GROUP * HD)
        pairs = [(ref.at[:, wide], rows.at[n, :, here]) for n, ref in enumerate((lq, lk, v, g))]
        pairs.append((fm.at[pl.ds(head, GROUP)], maps.at[step * GROUP : (step + 1) * GROUP]))
        return [
            pltpu.make_async_copy(source, target, arrived.at[step, n])
            for n, (source, target) in enumerate(pairs)
        ]

    started = [copies(step) for step in range(steps)]
    tails = [
        pltpu.make_async_copy(
            ref.at[pl.ds(ref.shape[0] - WINDOW, WINDOW)], ends.at[n], arrived.at[n, 5]
        )
        for n, ref in enumerate((wk, v) if ends_too else ())
    ]
    for copy in [copy for step in started for copy in step] + tails:
        copy.start()
    for step, arriving in enumerate(started):
        for copy in arriving:
            copy.wait()
        heads = range(step * GROUP, (step + 1) * GROUP)
        pre = [(dot(rows[0, :, col(h)], maps[h]), dot(rows[1, :, col(h)], maps[h])) for h in heads]
        feats = [(phi(q).astype(BF), phi(k).astype(BF)) for q, k in pre]
        for h, (fq, fk) in zip(heads, feats):
            fq_out[:, col(h)], fk_out[:, col(h)] = fq, fk
        sums = [
            (dot_tn(fk, rows[2, :, col(h)]), dot_tn(fq, rows[3, :, col(h)]))
            for h, (fq, fk) in zip(heads, feats)
        ]
        for h, (forward, backward) in zip(heads, sums):
            t_out[h // CHUNK][0, h % CHUNK] = forward.astype(BF)
            t_out[h // CHUNK][1, h % CHUNK] = backward.astype(BF)
    for copy in tails:
        copy.wait()


def dropped(kernel, at, *refs):
    kernel(*refs[:at], *refs[at + 1 :])


def features(first, count, ends_too, lq, lk, v, g, fm, wk, follows):
    tokens = lq.shape[0]
    row = array((tokens, count * CHUNK * HD), BF)
    outs = [row, row] + [array((2, CHUNK, HD, HD), BF)] * count
    operands = [pltpu.with_memory_space_constraint(x, pltpu.HBM) for x in (lq, lk, v, g, fm, wk)]
    kernel = functools.partial(feature_kernel, first, count, ends_too)
    if follows is not None:
        kernel = functools.partial(dropped, kernel, len(operands))
        operands.append(follows)
    return call(
        kernel,
        "features",
        outs + [array((2, WINDOW, WIDE), BF)] * ends_too,
        operands,
        in_hbm=6,
        unread=len(operands) - 6,
        scratch_shapes=[
            pltpu.VMEM((4, tokens, count * CHUNK * HD), BF),
            pltpu.VMEM((count * CHUNK, HD, HD), BF),
            pltpu.SemaphoreType.DMA((count * CHUNK // GROUP, 6)),
        ],
    )


def causal_mask(tokens):
    rows = lax.broadcasted_iota(jnp.int32, (tokens, tokens), 0)
    cols = lax.broadcasted_iota(jnp.int32, (tokens, tokens), 1)
    return rows >= cols


def window_kernel(wq, wk, v, g, rims, *rest):
    win, dv, dwq, dwk, edge = rest[-5:]
    tokens = wq.shape[0]
    root = HD ** (-0.5)
    rows = lax.broadcasted_iota(jnp.int32, (tokens, 2 * WINDOW), 0)
    cols = lax.broadcasted_iota(jnp.int32, (tokens, 2 * WINDOW), 1)
    offset = cols - rows % WINDOW
    absent = (lax.axis_index("seq") == 0) & (rows < WINDOW) & (cols < WINDOW)
    band = (offset >= 1) & (offset <= WINDOW) & jnp.logical_not(absent)
    blocks = range(tokens // WINDOW)

    def rows_of(block):
        return slice(block * WINDOW, (block + 1) * WINDOW)

    def pairs(ref, rim, c):
        first = jnp.concatenate([rims[rim, :, c], ref[:WINDOW, c]], axis=0)
        return [first] + [ref[(n - 1) * WINDOW : (n + 1) * WINDOW, c] for n in blocks[1:]]

    def by_block(form, lefts, rights):
        return jnp.concatenate([form(a, b) for a, b in zip(lefts, rights)], axis=0)

    for start in range(0, HEADS, WINDOW_GROUP):
        at = [col(h) for h in range(start, start + WINDOW_GROUP)]
        q = [[wq[rows_of(n), c] for n in blocks] for c in at]
        grad = [[g[rows_of(n), c] for n in blocks] for c in at]
        keys, vals = [pairs(wk, 0, c) for c in at], [pairs(v, 1, c) for c in at]
        score = [by_block(dot_nt, a, b) for a, b in zip(q, keys)]
        dprob = [by_block(dot_nt, a, b) for a, b in zip(grad, vals)]
        score = [jnp.where(band, x * root, -jnp.inf) for x in score]
        top = [jnp.max(x, axis=-1, keepdims=True) for x in score]
        expo = [jnp.exp(x - y) for x, y in zip(score, top)]
        prob = [x / jnp.sum(x, axis=-1, keepdims=True) for x in expo]
        delta = [jnp.sum(x * y, axis=-1, keepdims=True) for x, y in zip(prob, dprob)]
        dscore = [
            (x * (y - z) * root).astype(BF) for x, y, z in zip(prob, dprob, delta)
        ]
        prob = [x.astype(BF) for x in prob]
        prob = [[x[rows_of(n)] for n in blocks] for x in prob]
        dscore = [[x[rows_of(n)] for n in blocks] for x in dscore]
        for i, c in enumerate(at):
            win[:, c] = by_block(dot, prob[i], vals[i])
            dwq[:, c] = by_block(dot, dscore[i], keys[i]).astype(BF)
        for i, c in enumerate(at):
            dk = [dot_tn(x, y) for x, y in zip(dscore[i], q[i])]
            dval = [dot_tn(x, y) for x, y in zip(prob[i], grad[i])]
            edge[0, :, c], edge[1, :, c] = dk[0][:WINDOW].astype(BF), dval[0][:WINDOW].astype(BF)
            for n in blocks:
                more = n + 1 < len(blocks)
                a, b = dk[n][WINDOW:], dval[n][WINDOW:]
                dwk[rows_of(n), c] = a + dk[n + 1][:WINDOW] if more else a
                dv[rows_of(n), c] = b + dval[n + 1][:WINDOW] if more else b


def window_part(*operands):
    wide = array(operands[0].shape, F32)
    return call(
        window_kernel,
        "window_part",
        [wide, wide, array(wide.shape, BF), wide, array((2, WINDOW, WIDE), BF)],
        operands,
        unread=len(operands) - 5,
    )


def state_kernel(first, count, lq, lk, v, g, fq, fk, *rest):
    states, (dpq_out, dpk_out, keep, send) = rest[:count], rest[-4:]
    core, far = lax.axis_index("dp") % 2, lax.axis_index("dp") // 2
    side = 0 if count == CHUNKS else 1
    half = own_half() if side == 0 else 1 - own_half()
    scale = lin_scale(lq.shape[0])
    causal = causal_mask(lq.shape[0])
    if side == 1:
        keep[0], send[0] = rest[count][0], rest[count + 1][0]
        if first > 0:
            keep[1, :, :first] = rest[count][1, :, :first]
            send[1, :, :first] = rest[count + 1][1, :, :first]
    for n in range(count):
        heads = [(first + n) * CHUNK + h for h in range(CHUNK)]
        at = [col_of(half, head) for head in heads]
        local = [col(n * CHUNK + h) for h in range(CHUNK)]
        q_feat, k_feat = [fq[:, x] for x in local], [fk[:, x] for x in local]
        val, grad = [v[:, x] for x in at], [g[:, x] for x in at]
        mixed = [jnp.where(causal, dot_nt(a, b), 0.0).astype(BF) for a, b in zip(grad, val)]
        dfq = [dot_nt(a, states[n][0, h]) for h, a in enumerate(grad)]
        dfk = [dot_nt(a, states[n][1, h]) for h, a in enumerate(val)]
        dfq = [(a + dot(b, c)) * scale for a, b, c in zip(dfq, mixed, k_feat)]
        dfk = [(a + dot_tn(b, c)) * scale for a, b, c in zip(dfk, mixed, q_feat)]
        dpq = [(a * jnp.minimum(b.astype(F32), 1.0)).astype(BF) for a, b in zip(dfq, q_feat)]
        dpk = [(a * jnp.minimum(b.astype(F32), 1.0)).astype(BF) for a, b in zip(dfk, k_feat)]
        terms = [
            (dot_tn(lq[:, x], a) + dot_tn(lk[:, x], b)).astype(BF)
            for x, a, b in zip(at, dpq, dpk)
        ]
        for h in range(CHUNK):
            here = col(n * CHUNK + h)
            dpq_out[:, here], dpk_out[:, here] = dpq[h], dpk[h]
        for y in range(2):
            keep[side, y ^ far, first + n] = jnp.where(core == 0, terms[y], terms[2 + y])
            send[side, y ^ far, first + n] = jnp.where(core == 0, terms[2 + y], terms[y])


def state_part(first, count, arrays, states, earlier, follows=()):
    row = array((arrays[0].shape[0], count * CHUNK * HD), BF)
    part = array((2, 2, CHUNKS, HD, HD), BF)
    return call(
        functools.partial(state_kernel, first, count),
        "state_part",
        [row, row, part, part],
        (*arrays, *states, *earlier, *follows),
        unread=len(follows),
    )


def output_kernel(v, g, fm, win, dv_win, dq, dk, edge, *rest):
    att, dlq, dlk, dv, dwq, dwk, token = rest[-7:]
    token[...] = jnp.zeros_like(token)
    scale = lin_scale(v.shape[0])
    causal = causal_mask(v.shape[0])
    tail = v.shape[0] - WINDOW
    dwq[...] = dq[...]
    dwk[:tail] = dk[:tail].astype(BF)
    dwk[tail:] = (dk[tail:] + edge[0].astype(F32)).astype(BF)
    for side in range(2):
        half = own_half() ^ side
        refs = rest[: 4 + CHUNKS] if side == 0 else rest[4 + CHUNKS : -7]
        states, pairs = refs[:CHUNKS], refs[CHUNKS:]
        each = 4 * HALF // len(pairs)
        for n in range(CHUNKS):
            heads = [n * CHUNK + k for k in range(CHUNK)]
            cols = [(col(h % each), col_of(half, h)) for h in heads]
            fq, fk, dpq, dpk = pairs[4 * (n * CHUNK // each) :][:4]
            scores = [
                jnp.where(causal, dot_nt(fq[:, c], fk[:, c]), 0.0).astype(BF) for c, _ in cols
            ]
            for h, (_, at) in zip(heads, cols):
                here, w = col(h % each), fm[half * HALF + h]
                dlq[:, at] = dot_nt(dpq[:, here], w).astype(BF)
                dlk[:, at] = dot_nt(dpk[:, here], w).astype(BF)
            lin = [dot(fq[:, c], states[n][0, k]) for k, (c, _) in enumerate(cols)]
            grad_v = [dot(fk[:, c], states[n][1, k]) for k, (c, _) in enumerate(cols)]
            for k, (_, at) in enumerate(cols):
                out = (lin[k] + dot(scores[k], v[:, at])) * scale
                att[:, at] = (out + win[:, at]).astype(BF)
                out = (grad_v[k] + dot_tn(scores[k], g[:, at])) * scale + dv_win[:, at]
                dv[:tail, at] = out[:tail].astype(BF)
                dv[tail:, at] = (out[tail:] + edge[1, :, at].astype(F32)).astype(BF)


def output_part(v, g, fm, windows, own, other):
    row = array(v.shape, BF)
    return call(
        output_kernel, "output_part", [row] * 6 + [array((8, HD), F32)], (v, g, fm, *windows, *own, *other)
    )


def flipped(block, bit):
    count = lax.axis_size("seq")
    return lax.ppermute(block, "seq", [(i, i ^ bit) for i in range(count)])


def flat_flipped(block, seq_bits, dp_bits):
    rows, width = lax.axis_size("seq"), lax.axis_size("dp")
    route = [
        (s * width + d, (s ^ seq_bits) * width + (d ^ dp_bits))
        for s in range(rows)
        for d in range(width)
    ]
    return lax.ppermute(block, ("seq", "dp"), route)


def relayed(block):
    devices = range(1, lax.axis_size("seq") - 2, 2)
    return lax.ppermute(block, "seq", [(i, i + 2) for i in devices])


def relay_kernel(own, came, out):
    out[...] = jnp.where(own_half() == 1, came[...], own[...])


def relay(own, came):
    return call(relay_kernel, "relay", [array(own.shape, own.dtype)], (own, came))[0]


def passed_along(block, distance):
    devices = range(lax.axis_size("seq"))
    route = [(i - distance, i) for i in devices if i - distance in devices]
    return lax.ppermute(block, "seq", route)


def spread(block, level):
    count = lax.axis_size("seq")
    size = 2 << level
    arrived = []
    for turn in range(1 << level):
        route = []
        for base in range(0, count // 2, size):
            low, high = base + size // 2 - 1, base + size // 2
            for parity in range(2):
                route.append((2 * low + parity, 2 * (high + turn) + parity))
                route.append((2 * high + parity, 2 * (low - turn) + parity))
        arrived.append(lax.ppermute(block, "seq", route))
    return arrived


def levels():
    return (lax.axis_size("seq") // 2).bit_length() - 1


def upper(level):
    return ((lax.axis_index("seq") // 2) >> level) % 2 == 1


def sides(gots):
    low = high = None
    for level, arrived in enumerate(gots):
        got = sum(x[...].astype(F32) for x in arrived)
        above = upper(level)
        a, b = jnp.where(above, got, 0.0), jnp.where(above, 0.0, got)
        low, high = (a, b) if low is None else (low + a, high + b)
    return low, high


def by_level(refs):
    gots, at = [], 0
    while at < len(refs):
        count = 1 << len(gots)
        gots.append(refs[at : at + count])
        at += count
    return gots


def pair_kernel(kept, came, pair, send):
    total = kept[...].astype(F32) + came[...].astype(F32)
    pair[...] = total.astype(BF)
    send[...] = jnp.where(upper(0), total[1], total[0]).astype(BF)


def pair_sum(kept, came):
    return call(
        pair_kernel, "pair_sum", [array(kept.shape, BF), array(kept.shape[1:], BF)], (kept, came)
    )


def level_kernel(pair, *refs):
    *gots, send = refs
    gots = by_level(gots)
    low, high = sides(gots)
    above = upper(len(gots))
    send[...] = jnp.where(
        above, pair[1].astype(F32) + high, pair[0].astype(F32) + low
    ).astype(BF)


def level_sum(pair, gots):
    return call(level_kernel, "level_sum", [array(pair.shape[1:], BF)], (pair, *gots))[0]


def entering_kernel(kept, came, *refs):
    *gots, mine, others = refs
    low, high = sides(by_level(gots))
    zero = jnp.zeros_like(low)
    low, high = (zero, zero) if low is None else (low, high)
    first = own_half() == 0
    mine[0] = (low + jnp.where(first, zero, came[0].astype(F32))).astype(BF)
    mine[1] = (high + jnp.where(first, came[1].astype(F32), zero)).astype(BF)
    others[0] = (low + jnp.where(first, kept[0].astype(F32), zero)).astype(BF)
    others[1] = (high + jnp.where(first, zero, kept[1].astype(F32))).astype(BF)


def entering(kept, came, gots):
    return call(
        entering_kernel, "entering", [array(kept.shape, BF)] * 2, (kept, came, *gots)
    )


def near_kernel(keep, came, mine, a, b, c):
    def total(side, y):
        return keep[side, y].astype(F32) + came[side, y].astype(F32)

    mine[...] = total(0, 0)
    a[...], b[...], c[...] = (total(*at).astype(BF) for at in ((1, 0), (0, 1), (1, 1)))


def near_sum(keep, came):
    part = array(keep.shape[2:], BF)
    return call(
        near_kernel, "near_sum", [array(part.shape, F32), part, part, part], (keep, came)
    )


def total_kernel(count, *refs):
    refs[-1][...] = sum(x[...].astype(F32) for x in refs[:count]).astype(BF)


def total_of(arrays, follows=()):
    return call(
        functools.partial(total_kernel, len(arrays)),
        "total",
        [array(arrays[0].shape, BF)],
        (*arrays, *follows),
        unread=len(follows),
    )[0]


def assemble_kernel(norm, *refs):
    pieces, out = refs[:-1], refs[-1]
    core, far = lax.axis_index("dp") % 2, lax.axis_index("dp") // 2
    for side in range(2):
        half = own_half() ^ side
        for n in range(CHUNKS):
            for c in range(2):
                for y in range(2):
                    head = half * HALF + n * CHUNK + (c ^ core) * 2 + (y ^ far)
                    out[head] = pieces[side * 4 + c * 2 + y][n].astype(F32) * norm


def assemble(pieces, norm):
    return call(
        functools.partial(assemble_kernel, norm), "assemble", [array((HEADS, HD, HD), F32)], pieces
    )[0]


def on_device(
    linear_queries, linear_keys, window_queries, window_keys, values, cotangent, feature_map
):
    tokens = linear_queries.shape[1]
    total_tokens = tokens * lax.axis_size("seq") * lax.axis_size("dp") * linear_queries.shape[0]
    lq, lk, wq, wk, v, g = (
        x[0]
        for x in (linear_queries, linear_keys, window_queries, window_keys, values, cotangent)
    )
    rows = (lq, lk, v, g)
    inputs = (*rows, feature_map, wk)
    feats, came, last = [], [], None
    for n in range(CHUNKS):
        fq, fk, sums, *ends = features(n, 1, n == CHUNKS - 1, *inputs, last)
        last = fq
        feats.append((fq, fk))
        came.append(flipped(sums, 1))
    far_ends = relayed(ends[0])
    fq, fk, *kept = features(0, CHUNKS, False, *inputs, last)
    came[-1], far_ends = lax.optimization_barrier((came[-1], far_ends))
    rims = flipped(relay(ends[0], far_ends), 1)
    pair, sent = zip(*(pair_sum(a, b) for a, b in zip(kept, came)))
    pair, sent = list(pair), list(sent)
    gots = [[] for _ in range(CHUNKS)]
    for level in range(levels()):
        if level > 0:
            sent = [level_sum(pair[n], gots[n]) for n in range(CHUNKS)]
        for n in range(CHUNKS):
            gots[n] += spread(sent[n], level)
    mine, others = zip(*(entering(kept[n], came[n], gots[n]) for n in range(CHUNKS)))
    back = [flipped(x, 1) for x in others]
    *windows, edge = window_part(wq, wk, v, g, rims, others[-1])
    back, edge = lax.optimization_barrier((back, edge))
    edge = passed_along(edge, -1)
    dpq, dpk, *terms = state_part(0, CHUNKS, (*rows, fq, fk), mine, (), (others[-1],))
    own = (*mine, fq, fk, dpq, dpk)
    pairs = []
    for n in range(CHUNKS):
        dpq, dpk, *terms = state_part(n, 1, (*rows, *feats[n]), (back[n],), terms)
        pairs += [*feats[n], dpq, dpk]
    other = (*back, *pairs)
    keep, send = terms
    near, a, b, c = near_sum(keep, flat_flipped(send, 0, 1))
    a, b, c = flat_flipped(a, 1, 0), flat_flipped(b, 0, 2), flat_flipped(c, 1, 2)
    sent = total_of((near, a, b, c))
    came = [flat_flipped(sent, bits, 0) for bits in range(2, lax.axis_size("seq"), 2)]
    attended, dlq, dlk, dv, dwq, dwk, token = output_part(
        v, g, feature_map, (*windows, edge), own, other
    )
    done = total_of((sent, *came), (token,))
    a, b, c = flat_flipped(done, 1, 0), flat_flipped(done, 0, 2), flat_flipped(done, 1, 2)
    across = [flat_flipped(x, 0, 1) for x in (done, b, a, c)]
    map_grad = assemble(
        (done, b, *across[:2], a, c, *across[2:]), total_tokens ** (-0.5)
    )
    return attended[None], dlq[None], dlk[None], dwq[None], dwk[None], dv[None], map_grad


def solution(mesh):
    row = P("dp", "seq", None)
    return jax.shard_map(
        on_device,
        mesh=mesh,
        in_specs=(row,) * 6 + (P(),),
        out_specs=(row,) * 6 + (P(),),
        check_vma=False,
    )
```

```python
import functools

import jax
import jax.numpy as jnp
from jax import lax
from jax.experimental import pallas as pl
from jax.experimental.pallas import tpu as pltpu
from jax.sharding import PartitionSpec as P

HEADS = 16
HD = 128
WINDOW = 64
HALF = HEADS // 2
CHUNKS = 2
CHUNK = HALF // CHUNKS
GROUP = 2
WINDOW_GROUP = 4
WIDE = HEADS * HD
VMEM = 8 * 1024 * 1024
BF = jnp.bfloat16
F32 = jnp.float32


def dot(left, right):
    return jnp.dot(left, right, preferred_element_type=F32)


def dot_nt(left, right):
    return lax.dot_general(left, right, (((1,), (1,)), ((), ())), preferred_element_type=F32)


def dot_tn(left, right):
    return lax.dot_general(left, right, (((0,), (0,)), ((), ())), preferred_element_type=F32)


def phi(before):
    return jnp.where(before > 0, before + 1.0, jnp.exp(jnp.minimum(before, 0.0)))


def col(head):
    return slice(head * HD, (head + 1) * HD)


def col_of(half, head):
    return pl.ds(pl.multiple_of(half * (HALF * HD) + head * HD, HD), HD)


def own_half():
    return lax.axis_index("seq") % 2


def lin_scale(tokens):
    return 1.0 / (HD * tokens * lax.axis_size("seq"))


def cost(microseconds):
    return pl.CostEstimate(
        flops=int(microseconds * 1000), bytes_accessed=1000, transcendentals=0
    )


def array(shape, kind):
    return jax.ShapeDtypeStruct(shape, kind)


def call(kernel, name, outs, operands, in_hbm=0, unread=0, microseconds=3, **more):
    whole = pl.BlockSpec(memory_space=pltpu.VMEM)
    return pl.pallas_call(
        kernel,
        in_specs=[pl.BlockSpec(memory_space=pltpu.HBM)] * in_hbm
        + [whole] * (len(operands) - in_hbm - unread)
        + [pl.BlockSpec(memory_space=pl.ANY)] * unread,
        out_specs=[whole] * len(outs),
        out_shape=outs,
        cost_estimate=cost(microseconds),
        compiler_params=pltpu.CompilerParams(vmem_limit_bytes=VMEM),
        name=name,
        **more,
    )(*operands)


def feature_kernel(partner, lq, lk, v, g, fm, wk, *rest):
    fq_out, fk_out, *t_out, rows, maps, arrived = rest
    ends = t_out.pop() if partner else None
    half = 1 - own_half() if partner else own_half()
    steps = HALF // GROUP

    def copies(step):
        head = half * HALF + step * GROUP
        wide = pl.ds(pl.multiple_of(head * HD, GROUP * HD), GROUP * HD)
        here = slice(step * GROUP * HD, (step + 1) * GROUP * HD)
        pairs = [(ref.at[:, wide], rows.at[n, :, here]) for n, ref in enumerate((lq, lk, v, g))]
        pairs.append((fm.at[pl.ds(head, GROUP)], maps.at[step * GROUP : (step + 1) * GROUP]))
        return [
            pltpu.make_async_copy(source, target, arrived.at[step, n])
            for n, (source, target) in enumerate(pairs)
        ]

    started = [copies(step) for step in range(steps)]
    tails = [
        pltpu.make_async_copy(
            ref.at[pl.ds(ref.shape[0] - WINDOW, WINDOW)], ends.at[n], arrived.at[n, 5]
        )
        for n, ref in enumerate((wk, v) if partner else ())
    ]
    for copy in [copy for step in started for copy in step] + tails:
        copy.start()
    for step, arriving in enumerate(started):
        for copy in arriving:
            copy.wait()
        heads = range(step * GROUP, (step + 1) * GROUP)
        pre = [(dot(rows[0, :, col(h)], maps[h]), dot(rows[1, :, col(h)], maps[h])) for h in heads]
        feats = [(phi(q).astype(BF), phi(k).astype(BF)) for q, k in pre]
        for h, (fq, fk) in zip(heads, feats):
            fq_out[:, col(h)], fk_out[:, col(h)] = fq, fk
        sums = [
            (dot_tn(fk, rows[2, :, col(h)]), dot_tn(fq, rows[3, :, col(h)]))
            for h, (fq, fk) in zip(heads, feats)
        ]
        for h, (forward, backward) in zip(heads, sums):
            t_out[h // CHUNK][0, h % CHUNK] = forward.astype(BF)
            t_out[h // CHUNK][1, h % CHUNK] = backward.astype(BF)
    for copy in tails:
        copy.wait()


def dropped(kernel, at, *refs):
    kernel(*refs[:at], *refs[at + 1 :])


def features(lq, lk, v, g, fm, wk, follows):
    tokens = lq.shape[0]
    partner = follows is None
    row = array((tokens, HALF * HD), BF)
    outs = [row, row] + [array((2, CHUNK, HD, HD), BF)] * CHUNKS
    operands = [pltpu.with_memory_space_constraint(x, pltpu.HBM) for x in (lq, lk, v, g, fm, wk)]
    kernel = functools.partial(feature_kernel, partner)
    if not partner:
        kernel = functools.partial(dropped, kernel, len(operands))
        operands.append(follows)
    return call(
        kernel,
        "features",
        outs + [array((2, WINDOW, WIDE), BF)] * partner,
        operands,
        in_hbm=6,
        unread=len(operands) - 6,
        scratch_shapes=[
            pltpu.VMEM((4, tokens, HALF * HD), BF),
            pltpu.VMEM((HALF, HD, HD), BF),
            pltpu.SemaphoreType.DMA((HALF // GROUP, 6)),
        ],
    )


def causal_mask(tokens):
    rows = lax.broadcasted_iota(jnp.int32, (tokens, tokens), 0)
    cols = lax.broadcasted_iota(jnp.int32, (tokens, tokens), 1)
    return rows >= cols


def window_kernel(wq, wk, v, g, rims, *rest):
    win, dv, dwq, dwk, edge = rest[-5:]
    tokens = wq.shape[0]
    root = HD ** (-0.5)
    rows = lax.broadcasted_iota(jnp.int32, (tokens, 2 * WINDOW), 0)
    cols = lax.broadcasted_iota(jnp.int32, (tokens, 2 * WINDOW), 1)
    offset = cols - rows % WINDOW
    absent = (lax.axis_index("seq") == 0) & (rows < WINDOW) & (cols < WINDOW)
    band = (offset >= 1) & (offset <= WINDOW) & jnp.logical_not(absent)
    blocks = range(tokens // WINDOW)

    def rows_of(block):
        return slice(block * WINDOW, (block + 1) * WINDOW)

    def pairs(ref, rim, c):
        first = jnp.concatenate([rims[rim, :, c], ref[:WINDOW, c]], axis=0)
        return [first] + [ref[(n - 1) * WINDOW : (n + 1) * WINDOW, c] for n in blocks[1:]]

    def by_block(form, lefts, rights):
        return jnp.concatenate([form(a, b) for a, b in zip(lefts, rights)], axis=0)

    for start in range(0, HEADS, WINDOW_GROUP):
        at = [col(h) for h in range(start, start + WINDOW_GROUP)]
        q = [[wq[rows_of(n), c] for n in blocks] for c in at]
        grad = [[g[rows_of(n), c] for n in blocks] for c in at]
        keys, vals = [pairs(wk, 0, c) for c in at], [pairs(v, 1, c) for c in at]
        score = [by_block(dot_nt, a, b) for a, b in zip(q, keys)]
        dprob = [by_block(dot_nt, a, b) for a, b in zip(grad, vals)]
        score = [jnp.where(band, x * root, -jnp.inf) for x in score]
        top = [jnp.max(x, axis=-1, keepdims=True) for x in score]
        expo = [jnp.exp(x - y) for x, y in zip(score, top)]
        prob = [x / jnp.sum(x, axis=-1, keepdims=True) for x in expo]
        delta = [jnp.sum(x * y, axis=-1, keepdims=True) for x, y in zip(prob, dprob)]
        dscore = [
            (x * (y - z) * root).astype(BF) for x, y, z in zip(prob, dprob, delta)
        ]
        prob = [x.astype(BF) for x in prob]
        prob = [[x[rows_of(n)] for n in blocks] for x in prob]
        dscore = [[x[rows_of(n)] for n in blocks] for x in dscore]
        for i, c in enumerate(at):
            win[:, c] = by_block(dot, prob[i], vals[i])
            dwq[:, c] = by_block(dot, dscore[i], keys[i]).astype(BF)
        for i, c in enumerate(at):
            dk = [dot_tn(x, y) for x, y in zip(dscore[i], q[i])]
            dval = [dot_tn(x, y) for x, y in zip(prob[i], grad[i])]
            edge[0, :, c], edge[1, :, c] = dk[0][:WINDOW].astype(BF), dval[0][:WINDOW].astype(BF)
            for n in blocks:
                more = n + 1 < len(blocks)
                a, b = dk[n][WINDOW:], dval[n][WINDOW:]
                dwk[rows_of(n), c] = a + dk[n + 1][:WINDOW] if more else a
                dv[rows_of(n), c] = b + dval[n + 1][:WINDOW] if more else b


def window_part(*operands):
    wide = array(operands[0].shape, F32)
    return call(
        window_kernel,
        "window_part",
        [wide, wide, array(wide.shape, BF), wide, array((2, WINDOW, WIDE), BF)],
        operands,
        unread=len(operands) - 5,
    )


def state_kernel(first, count, lq, lk, v, g, fq, fk, *rest):
    states, (dpq_out, dpk_out, keep, send) = rest[:count], rest[-4:]
    core, far = lax.axis_index("dp") % 2, lax.axis_index("dp") // 2
    side = 0 if count == CHUNKS else 1
    half = own_half() if side == 0 else 1 - own_half()
    scale = lin_scale(lq.shape[0])
    causal = causal_mask(lq.shape[0])
    if side == 1:
        keep[...], send[...] = rest[count][...], rest[count + 1][...]
    for n in range(count):
        heads = [(first + n) * CHUNK + h for h in range(CHUNK)]
        at = [col_of(half, head) for head in heads]
        q_feat, k_feat = [fq[:, col(x)] for x in heads], [fk[:, col(x)] for x in heads]
        val, grad = [v[:, x] for x in at], [g[:, x] for x in at]
        mixed = [jnp.where(causal, dot_nt(a, b), 0.0).astype(BF) for a, b in zip(grad, val)]
        dfq = [dot_nt(a, states[n][0, h]) for h, a in enumerate(grad)]
        dfk = [dot_nt(a, states[n][1, h]) for h, a in enumerate(val)]
        dfq = [(a + dot(b, c)) * scale for a, b, c in zip(dfq, mixed, k_feat)]
        dfk = [(a + dot_tn(b, c)) * scale for a, b, c in zip(dfk, mixed, q_feat)]
        dpq = [(a * jnp.minimum(b.astype(F32), 1.0)).astype(BF) for a, b in zip(dfq, q_feat)]
        dpk = [(a * jnp.minimum(b.astype(F32), 1.0)).astype(BF) for a, b in zip(dfk, k_feat)]
        terms = [
            (dot_tn(lq[:, x], a) + dot_tn(lk[:, x], b)).astype(BF)
            for x, a, b in zip(at, dpq, dpk)
        ]
        for h in range(CHUNK):
            here = col(n * CHUNK + h)
            dpq_out[:, here], dpk_out[:, here] = dpq[h], dpk[h]
        for y in range(2):
            keep[side, y ^ far, first + n] = jnp.where(core == 0, terms[y], terms[2 + y])
            send[side, y ^ far, first + n] = jnp.where(core == 0, terms[2 + y], terms[y])


def state_part(first, count, arrays, states, earlier, follows=()):
    row = array((arrays[0].shape[0], count * CHUNK * HD), BF)
    part = array((2, 2, CHUNKS, HD, HD), BF)
    return call(
        functools.partial(state_kernel, first, count),
        "state_part",
        [row, row, part, part],
        (*arrays, *states, *earlier, *follows),
        unread=len(follows),
    )


def output_kernel(v, g, fm, win, dv_win, dq, dk, edge, *rest):
    att, dlq, dlk, dv, dwq, dwk, token = rest[-7:]
    token[...] = jnp.zeros_like(token)
    scale = lin_scale(v.shape[0])
    causal = causal_mask(v.shape[0])
    tail = v.shape[0] - WINDOW
    dwq[...] = dq[...]
    dwk[:tail] = dk[:tail].astype(BF)
    dwk[tail:] = (dk[tail:] + edge[0].astype(F32)).astype(BF)
    for side in range(2):
        half = own_half() ^ side
        refs = rest[: 4 + CHUNKS] if side == 0 else rest[4 + CHUNKS : -7]
        states, (fq, fk, *pairs) = refs[:CHUNKS], refs[CHUNKS:]
        each = 2 * HALF // len(pairs)
        for n in range(CHUNKS):
            heads = [n * CHUNK + k for k in range(CHUNK)]
            cols = [(col(h), col_of(half, h)) for h in heads]
            dpq, dpk = pairs[2 * (n * CHUNK // each) :][:2]
            scores = [
                jnp.where(causal, dot_nt(fq[:, c], fk[:, c]), 0.0).astype(BF) for c, _ in cols
            ]
            for h, (_, at) in zip(heads, cols):
                here, w = col(h % each), fm[half * HALF + h]
                dlq[:, at] = dot_nt(dpq[:, here], w).astype(BF)
                dlk[:, at] = dot_nt(dpk[:, here], w).astype(BF)
            lin = [dot(fq[:, c], states[n][0, k]) for k, (c, _) in enumerate(cols)]
            grad_v = [dot(fk[:, c], states[n][1, k]) for k, (c, _) in enumerate(cols)]
            for k, (_, at) in enumerate(cols):
                out = (lin[k] + dot(scores[k], v[:, at])) * scale
                att[:, at] = (out + win[:, at]).astype(BF)
                out = (grad_v[k] + dot_tn(scores[k], g[:, at])) * scale + dv_win[:, at]
                dv[:tail, at] = out[:tail].astype(BF)
                dv[tail:, at] = (out[tail:] + edge[1, :, at].astype(F32)).astype(BF)


def output_part(v, g, fm, windows, own, other):
    row = array(v.shape, BF)
    return call(
        output_kernel, "output_part", [row] * 6 + [array((8, HD), F32)], (v, g, fm, *windows, *own, *other)
    )


def flipped(block, bit):
    count = lax.axis_size("seq")
    return lax.ppermute(block, "seq", [(i, i ^ bit) for i in range(count)])


def flat_flipped(block, seq_bits, dp_bits):
    rows, width = lax.axis_size("seq"), lax.axis_size("dp")
    route = [
        (s * width + d, (s ^ seq_bits) * width + (d ^ dp_bits))
        for s in range(rows)
        for d in range(width)
    ]
    return lax.ppermute(block, ("seq", "dp"), route)


def relayed(block):
    devices = range(1, lax.axis_size("seq") - 2, 2)
    return lax.ppermute(block, "seq", [(i, i + 2) for i in devices])


def relay_kernel(own, came, out):
    out[...] = jnp.where(own_half() == 1, came[...], own[...])


def relay(own, came):
    return call(relay_kernel, "relay", [array(own.shape, own.dtype)], (own, came))[0]


def passed_along(block, distance):
    devices = range(lax.axis_size("seq"))
    route = [(i - distance, i) for i in devices if i - distance in devices]
    return lax.ppermute(block, "seq", route)


def spread(block, level):
    count = lax.axis_size("seq")
    size = 2 << level
    arrived = []
    for turn in range(1 << level):
        route = []
        for base in range(0, count // 2, size):
            low, high = base + size // 2 - 1, base + size // 2
            for parity in range(2):
                route.append((2 * low + parity, 2 * (high + turn) + parity))
                route.append((2 * high + parity, 2 * (low - turn) + parity))
        arrived.append(lax.ppermute(block, "seq", route))
    return arrived


def levels():
    return (lax.axis_size("seq") // 2).bit_length() - 1


def upper(level):
    return ((lax.axis_index("seq") // 2) >> level) % 2 == 1


def sides(gots):
    low = high = None
    for level, arrived in enumerate(gots):
        got = sum(x[...].astype(F32) for x in arrived)
        above = upper(level)
        a, b = jnp.where(above, got, 0.0), jnp.where(above, 0.0, got)
        low, high = (a, b) if low is None else (low + a, high + b)
    return low, high


def by_level(refs):
    gots, at = [], 0
    while at < len(refs):
        count = 1 << len(gots)
        gots.append(refs[at : at + count])
        at += count
    return gots


def pair_kernel(kept, came, pair, send):
    total = kept[...].astype(F32) + came[...].astype(F32)
    pair[...] = total.astype(BF)
    send[...] = jnp.where(upper(0), total[1], total[0]).astype(BF)


def pair_sum(kept, came):
    return call(
        pair_kernel, "pair_sum", [array(kept.shape, BF), array(kept.shape[1:], BF)], (kept, came)
    )


def level_kernel(pair, *refs):
    *gots, send = refs
    gots = by_level(gots)
    low, high = sides(gots)
    above = upper(len(gots))
    send[...] = jnp.where(
        above, pair[1].astype(F32) + high, pair[0].astype(F32) + low
    ).astype(BF)


def level_sum(pair, gots):
    return call(level_kernel, "level_sum", [array(pair.shape[1:], BF)], (pair, *gots))[0]


def entering_kernel(kept, came, *refs):
    *gots, mine, others = refs
    low, high = sides(by_level(gots))
    zero = jnp.zeros_like(low)
    low, high = (zero, zero) if low is None else (low, high)
    first = own_half() == 0
    mine[0] = (low + jnp.where(first, zero, came[0].astype(F32))).astype(BF)
    mine[1] = (high + jnp.where(first, came[1].astype(F32), zero)).astype(BF)
    others[0] = (low + jnp.where(first, kept[0].astype(F32), zero)).astype(BF)
    others[1] = (high + jnp.where(first, zero, kept[1].astype(F32))).astype(BF)


def entering(kept, came, gots):
    return call(
        entering_kernel, "entering", [array(kept.shape, BF)] * 2, (kept, came, *gots)
    )


def near_kernel(keep, came, mine, a, b, c):
    def total(side, y):
        return keep[side, y].astype(F32) + came[side, y].astype(F32)

    mine[...] = total(0, 0)
    a[...], b[...], c[...] = (total(*at).astype(BF) for at in ((1, 0), (0, 1), (1, 1)))


def near_sum(keep, came):
    part = array(keep.shape[2:], BF)
    return call(
        near_kernel, "near_sum", [array(part.shape, F32), part, part, part], (keep, came)
    )


def total_kernel(count, *refs):
    refs[-1][...] = sum(x[...].astype(F32) for x in refs[:count]).astype(BF)


def total_of(arrays, follows=()):
    return call(
        functools.partial(total_kernel, len(arrays)),
        "total",
        [array(arrays[0].shape, BF)],
        (*arrays, *follows),
        unread=len(follows),
    )[0]


def assemble_kernel(norm, *refs):
    pieces, out = refs[:-1], refs[-1]
    core, far = lax.axis_index("dp") % 2, lax.axis_index("dp") // 2
    for side in range(2):
        half = own_half() ^ side
        for n in range(CHUNKS):
            for c in range(2):
                for y in range(2):
                    head = half * HALF + n * CHUNK + (c ^ core) * 2 + (y ^ far)
                    out[head] = pieces[side * 4 + c * 2 + y][n].astype(F32) * norm


def assemble(pieces, norm):
    return call(
        functools.partial(assemble_kernel, norm), "assemble", [array((HEADS, HD, HD), F32)], pieces
    )[0]


def on_device(
    linear_queries, linear_keys, window_queries, window_keys, values, cotangent, feature_map
):
    tokens = linear_queries.shape[1]
    total_tokens = tokens * lax.axis_size("seq") * lax.axis_size("dp") * linear_queries.shape[0]
    lq, lk, wq, wk, v, g = (
        x[0]
        for x in (linear_queries, linear_keys, window_queries, window_keys, values, cotangent)
    )
    rows = (lq, lk, v, g)
    inputs = (*rows, feature_map, wk)
    fq_o, fk_o, *given, ends = features(*inputs, None)
    came = [flipped(x, 1) for x in given]
    far_ends = relayed(ends)
    fq, fk, *kept = features(*inputs, fq_o)
    came[-1], far_ends = lax.optimization_barrier((came[-1], far_ends))
    rims = flipped(relay(ends, far_ends), 1)
    pair, sent = zip(*(pair_sum(a, b) for a, b in zip(kept, came)))
    pair, sent = list(pair), list(sent)
    gots = [[] for _ in range(CHUNKS)]
    for level in range(levels()):
        if level > 0:
            sent = [level_sum(pair[n], gots[n]) for n in range(CHUNKS)]
        for n in range(CHUNKS):
            gots[n] += spread(sent[n], level)
    mine, others = zip(*(entering(kept[n], came[n], gots[n]) for n in range(CHUNKS)))
    back = [flipped(x, 1) for x in others]
    *windows, edge = window_part(wq, wk, v, g, rims, others[-1])
    dpq, dpk, *terms = state_part(0, CHUNKS, (*rows, fq, fk), mine, (), (others[-1],))
    own = (*mine, fq, fk, dpq, dpk)
    back[0], edge, terms = lax.optimization_barrier((back[0], edge, terms))
    edge = passed_along(edge, -1)
    pairs = [None] * CHUNKS
    for n in reversed(range(CHUNKS)):
        *pairs[n], keep, send = state_part(n, 1, (*rows, fq_o, fk_o), (back[n],), terms)
        terms = (keep, send)
    other = (*back, fq_o, fk_o, *(x for pair in pairs for x in pair))
    keep, send = terms
    near, a, b, c = near_sum(keep, flat_flipped(send, 0, 1))
    a, b, c = flat_flipped(a, 1, 0), flat_flipped(b, 0, 2), flat_flipped(c, 1, 2)
    sent = total_of((near, a, b, c))
    came = [flat_flipped(sent, bits, 0) for bits in range(2, lax.axis_size("seq"), 2)]
    attended, dlq, dlk, dv, dwq, dwk, token = output_part(
        v, g, feature_map, (*windows, edge), own, other
    )
    done = total_of((sent, *came), (token,))
    a, b, c = flat_flipped(done, 1, 0), flat_flipped(done, 0, 2), flat_flipped(done, 1, 2)
    across = [flat_flipped(x, 0, 1) for x in (done, b, a, c)]
    map_grad = assemble(
        (done, b, *across[:2], a, c, *across[2:]), total_tokens ** (-0.5)
    )
    return attended[None], dlq[None], dlk[None], dwq[None], dwk[None], dv[None], map_grad


def solution(mesh):
    row = P("dp", "seq", None)
    return jax.shard_map(
        on_device,
        mesh=mesh,
        in_specs=(row,) * 6 + (P(),),
        out_specs=(row,) * 6 + (P(),),
        check_vma=False,
    )
```

```python
import functools

import jax
import jax.numpy as jnp
from jax import lax
from jax.experimental import pallas as pl
from jax.experimental.pallas import tpu as pltpu
from jax.sharding import PartitionSpec as P

HEADS = 16
HD = 128
WINDOW = 64
HALF = HEADS // 2
CHUNKS = 2
CHUNK = HALF // CHUNKS
GROUP = 4
WINDOW_GROUP = 4
WIDE = HEADS * HD
VMEM = 8 * 1024 * 1024
BF = jnp.bfloat16
F32 = jnp.float32


def dot(left, right):
    return jnp.dot(left, right, preferred_element_type=F32)


def dot_nt(left, right):
    return lax.dot_general(left, right, (((1,), (1,)), ((), ())), preferred_element_type=F32)


def dot_tn(left, right):
    return lax.dot_general(left, right, (((0,), (0,)), ((), ())), preferred_element_type=F32)


def phi(before):
    return jnp.where(before > 0, before + 1.0, jnp.exp(jnp.minimum(before, 0.0)))


def col(head):
    return slice(head * HD, (head + 1) * HD)


def col_of(half, head):
    return pl.ds(pl.multiple_of(half * (HALF * HD) + head * HD, HD), HD)


def own_half():
    return lax.axis_index("seq") % 2


def lin_scale(tokens):
    return 1.0 / (HD * tokens * lax.axis_size("seq"))


def cost(microseconds):
    return pl.CostEstimate(
        flops=int(microseconds * 1000), bytes_accessed=1000, transcendentals=0
    )


def array(shape, kind):
    return jax.ShapeDtypeStruct(shape, kind)


def call(kernel, name, outs, operands, in_hbm=0, unread=0, microseconds=3, **more):
    whole = pl.BlockSpec(memory_space=pltpu.VMEM)
    return pl.pallas_call(
        kernel,
        in_specs=[pl.BlockSpec(memory_space=pltpu.HBM)] * in_hbm
        + [whole] * (len(operands) - in_hbm - unread)
        + [pl.BlockSpec(memory_space=pl.ANY)] * unread,
        out_specs=[whole] * len(outs),
        out_shape=outs,
        cost_estimate=cost(microseconds),
        compiler_params=pltpu.CompilerParams(vmem_limit_bytes=VMEM),
        name=name,
        **more,
    )(*operands)


def feature_kernel(partner, lq, lk, v, g, fm, wk, *rest):
    fq_out, fk_out, *t_out, rows, maps, arrived = rest
    ends = t_out.pop() if partner else None
    half = 1 - own_half() if partner else own_half()
    steps = HALF // GROUP

    def copies(step):
        head = half * HALF + step * GROUP
        wide = pl.ds(pl.multiple_of(head * HD, GROUP * HD), GROUP * HD)
        here = slice(step * GROUP * HD, (step + 1) * GROUP * HD)
        pairs = [(ref.at[:, wide], rows.at[n, :, here]) for n, ref in enumerate((lq, lk, v, g))]
        pairs.append((fm.at[pl.ds(head, GROUP)], maps.at[step * GROUP : (step + 1) * GROUP]))
        return [
            pltpu.make_async_copy(source, target, arrived.at[step, n])
            for n, (source, target) in enumerate(pairs)
        ]

    started = [copies(step) for step in range(steps)]
    tails = [
        pltpu.make_async_copy(
            ref.at[pl.ds(ref.shape[0] - WINDOW, WINDOW)], ends.at[n], arrived.at[n, 5]
        )
        for n, ref in enumerate((wk, v) if partner else ())
    ]
    for copy in [copy for step in started for copy in step] + tails:
        copy.start()
    for step, arriving in enumerate(started):
        for copy in arriving:
            copy.wait()
        heads = range(step * GROUP, (step + 1) * GROUP)
        pre = [(dot(rows[0, :, col(h)], maps[h]), dot(rows[1, :, col(h)], maps[h])) for h in heads]
        feats = [(phi(q).astype(BF), phi(k).astype(BF)) for q, k in pre]
        for h, (fq, fk) in zip(heads, feats):
            fq_out[:, col(h)], fk_out[:, col(h)] = fq, fk
        sums = [
            (dot_tn(fk, rows[2, :, col(h)]), dot_tn(fq, rows[3, :, col(h)]))
            for h, (fq, fk) in zip(heads, feats)
        ]
        for h, (forward, backward) in zip(heads, sums):
            t_out[h // CHUNK][0, h % CHUNK] = forward.astype(BF)
            t_out[h // CHUNK][1, h % CHUNK] = backward.astype(BF)
    for copy in tails:
        copy.wait()


def dropped(kernel, at, *refs):
    kernel(*refs[:at], *refs[at + 1 :])


def features(lq, lk, v, g, fm, wk, follows):
    tokens = lq.shape[0]
    partner = follows is None
    row = array((tokens, HALF * HD), BF)
    outs = [row, row] + [array((2, CHUNK, HD, HD), BF)] * CHUNKS
    operands = [pltpu.with_memory_space_constraint(x, pltpu.HBM) for x in (lq, lk, v, g, fm, wk)]
    kernel = functools.partial(feature_kernel, partner)
    if not partner:
        kernel = functools.partial(dropped, kernel, len(operands))
        operands.append(follows)
    return call(
        kernel,
        "features",
        outs + [array((2, WINDOW, WIDE), BF)] * partner,
        operands,
        in_hbm=6,
        unread=len(operands) - 6,
        scratch_shapes=[
            pltpu.VMEM((4, tokens, HALF * HD), BF),
            pltpu.VMEM((HALF, HD, HD), BF),
            pltpu.SemaphoreType.DMA((HALF // GROUP, 6)),
        ],
    )


def causal_mask(tokens):
    rows = lax.broadcasted_iota(jnp.int32, (tokens, tokens), 0)
    cols = lax.broadcasted_iota(jnp.int32, (tokens, tokens), 1)
    return rows >= cols


def window_kernel(wq, wk, v, g, rims, *rest):
    win, dv, dwq, dwk, edge = rest[-5:]
    tokens = wq.shape[0]
    root = HD ** (-0.5)
    rows = lax.broadcasted_iota(jnp.int32, (tokens, 2 * WINDOW), 0)
    cols = lax.broadcasted_iota(jnp.int32, (tokens, 2 * WINDOW), 1)
    offset = cols - rows % WINDOW
    absent = (lax.axis_index("seq") == 0) & (rows < WINDOW) & (cols < WINDOW)
    band = (offset >= 1) & (offset <= WINDOW) & jnp.logical_not(absent)
    blocks = range(tokens // WINDOW)

    def rows_of(block):
        return slice(block * WINDOW, (block + 1) * WINDOW)

    def pairs(ref, rim, c):
        first = jnp.concatenate([rims[rim, :, c], ref[:WINDOW, c]], axis=0)
        return [first] + [ref[(n - 1) * WINDOW : (n + 1) * WINDOW, c] for n in blocks[1:]]

    def by_block(form, lefts, rights):
        return jnp.concatenate([form(a, b) for a, b in zip(lefts, rights)], axis=0)

    for start in range(0, HEADS, WINDOW_GROUP):
        at = [col(h) for h in range(start, start + WINDOW_GROUP)]
        q = [[wq[rows_of(n), c] for n in blocks] for c in at]
        grad = [[g[rows_of(n), c] for n in blocks] for c in at]
        keys, vals = [pairs(wk, 0, c) for c in at], [pairs(v, 1, c) for c in at]
        score = [by_block(dot_nt, a, b) for a, b in zip(q, keys)]
        dprob = [by_block(dot_nt, a, b) for a, b in zip(grad, vals)]
        score = [jnp.where(band, x * root, -jnp.inf) for x in score]
        top = [jnp.max(x, axis=-1, keepdims=True) for x in score]
        expo = [jnp.exp(x - y) for x, y in zip(score, top)]
        prob = [x / jnp.sum(x, axis=-1, keepdims=True) for x in expo]
        delta = [jnp.sum(x * y, axis=-1, keepdims=True) for x, y in zip(prob, dprob)]
        dscore = [
            (x * (y - z) * root).astype(BF) for x, y, z in zip(prob, dprob, delta)
        ]
        prob = [x.astype(BF) for x in prob]
        prob = [[x[rows_of(n)] for n in blocks] for x in prob]
        dscore = [[x[rows_of(n)] for n in blocks] for x in dscore]
        for i, c in enumerate(at):
            win[:, c] = by_block(dot, prob[i], vals[i])
            dwq[:, c] = by_block(dot, dscore[i], keys[i]).astype(BF)
        for i, c in enumerate(at):
            dk = [dot_tn(x, y) for x, y in zip(dscore[i], q[i])]
            dval = [dot_tn(x, y) for x, y in zip(prob[i], grad[i])]
            edge[0, :, c], edge[1, :, c] = dk[0][:WINDOW].astype(BF), dval[0][:WINDOW].astype(BF)
            for n in blocks:
                more = n + 1 < len(blocks)
                a, b = dk[n][WINDOW:], dval[n][WINDOW:]
                dwk[rows_of(n), c] = a + dk[n + 1][:WINDOW] if more else a
                dv[rows_of(n), c] = b + dval[n + 1][:WINDOW] if more else b


def window_part(*operands):
    wide = array(operands[0].shape, F32)
    return call(
        window_kernel,
        "window_part",
        [wide, wide, array(wide.shape, BF), wide, array((2, WINDOW, WIDE), BF)],
        operands,
        unread=len(operands) - 5,
    )


def state_kernel(first, count, lq, lk, v, g, fq, fk, *rest):
    states, (dpq_out, dpk_out, keep, send) = rest[:count], rest[-4:]
    core, far = lax.axis_index("dp") % 2, lax.axis_index("dp") // 2
    side = 0 if count == CHUNKS else 1
    half = own_half() if side == 0 else 1 - own_half()
    scale = lin_scale(lq.shape[0])
    causal = causal_mask(lq.shape[0])
    if side == 1:
        keep[...], send[...] = rest[count][...], rest[count + 1][...]
    for n in range(count):
        heads = [(first + n) * CHUNK + h for h in range(CHUNK)]
        at = [col_of(half, head) for head in heads]
        q_feat, k_feat = [fq[:, col(x)] for x in heads], [fk[:, col(x)] for x in heads]
        val, grad = [v[:, x] for x in at], [g[:, x] for x in at]
        mixed = [jnp.where(causal, dot_nt(a, b), 0.0).astype(BF) for a, b in zip(grad, val)]
        dfq = [dot_nt(a, states[n][0, h]) for h, a in enumerate(grad)]
        dfk = [dot_nt(a, states[n][1, h]) for h, a in enumerate(val)]
        dfq = [(a + dot(b, c)) * scale for a, b, c in zip(dfq, mixed, k_feat)]
        dfk = [(a + dot_tn(b, c)) * scale for a, b, c in zip(dfk, mixed, q_feat)]
        dpq = [(a * jnp.minimum(b.astype(F32), 1.0)).astype(BF) for a, b in zip(dfq, q_feat)]
        dpk = [(a * jnp.minimum(b.astype(F32), 1.0)).astype(BF) for a, b in zip(dfk, k_feat)]
        terms = [
            (dot_tn(lq[:, x], a) + dot_tn(lk[:, x], b)).astype(BF)
            for x, a, b in zip(at, dpq, dpk)
        ]
        for h in range(CHUNK):
            here = col(n * CHUNK + h)
            dpq_out[:, here], dpk_out[:, here] = dpq[h], dpk[h]
        for y in range(2):
            keep[side, y ^ far, first + n] = jnp.where(core == 0, terms[y], terms[2 + y])
            send[side, y ^ far, first + n] = jnp.where(core == 0, terms[2 + y], terms[y])


def state_part(first, count, arrays, states, earlier, follows=()):
    row = array((arrays[0].shape[0], count * CHUNK * HD), BF)
    part = array((2, 2, CHUNKS, HD, HD), BF)
    return call(
        functools.partial(state_kernel, first, count),
        "state_part",
        [row, row, part, part],
        (*arrays, *states, *earlier, *follows),
        unread=len(follows),
    )


def output_kernel(v, g, fm, win, dv_win, dq, dk, edge, *rest):
    att, dlq, dlk, dv, dwq, dwk, token = rest[-7:]
    token[...] = jnp.zeros_like(token)
    scale = lin_scale(v.shape[0])
    causal = causal_mask(v.shape[0])
    tail = v.shape[0] - WINDOW
    dwq[...] = dq[...]
    dwk[:tail] = dk[:tail].astype(BF)
    dwk[tail:] = (dk[tail:] + edge[0].astype(F32)).astype(BF)
    for side in range(2):
        half = own_half() ^ side
        refs = rest[: 4 + CHUNKS] if side == 0 else rest[4 + CHUNKS : -7]
        states, (fq, fk, *pairs) = refs[:CHUNKS], refs[CHUNKS:]
        each = 2 * HALF // len(pairs)
        for n in range(CHUNKS):
            heads = [n * CHUNK + k for k in range(CHUNK)]
            cols = [(col(h), col_of(half, h)) for h in heads]
            dpq, dpk = pairs[2 * (n * CHUNK // each) :][:2]
            scores = [
                jnp.where(causal, dot_nt(fq[:, c], fk[:, c]), 0.0).astype(BF) for c, _ in cols
            ]
            for h, (_, at) in zip(heads, cols):
                here, w = col(h % each), fm[half * HALF + h]
                dlq[:, at] = dot_nt(dpq[:, here], w).astype(BF)
                dlk[:, at] = dot_nt(dpk[:, here], w).astype(BF)
            lin = [dot(fq[:, c], states[n][0, k]) for k, (c, _) in enumerate(cols)]
            grad_v = [dot(fk[:, c], states[n][1, k]) for k, (c, _) in enumerate(cols)]
            for k, (_, at) in enumerate(cols):
                out = (lin[k] + dot(scores[k], v[:, at])) * scale
                att[:, at] = (out + win[:, at]).astype(BF)
                out = (grad_v[k] + dot_tn(scores[k], g[:, at])) * scale + dv_win[:, at]
                dv[:tail, at] = out[:tail].astype(BF)
                dv[tail:, at] = (out[tail:] + edge[1, :, at].astype(F32)).astype(BF)


def output_part(v, g, fm, windows, own, other):
    row = array(v.shape, BF)
    return call(
        output_kernel, "output_part", [row] * 6 + [array((8, HD), F32)], (v, g, fm, *windows, *own, *other)
    )


def flipped(block, bit):
    count = lax.axis_size("seq")
    return lax.ppermute(block, "seq", [(i, i ^ bit) for i in range(count)])


def flat_flipped(block, seq_bits, dp_bits):
    rows, width = lax.axis_size("seq"), lax.axis_size("dp")
    route = [
        (s * width + d, (s ^ seq_bits) * width + (d ^ dp_bits))
        for s in range(rows)
        for d in range(width)
    ]
    return lax.ppermute(block, ("seq", "dp"), route)


def relayed(block):
    devices = range(1, lax.axis_size("seq") - 2, 2)
    return lax.ppermute(block, "seq", [(i, i + 2) for i in devices])


def relay_kernel(own, came, out):
    out[...] = jnp.where(own_half() == 1, came[...], own[...])


def relay(own, came):
    return call(relay_kernel, "relay", [array(own.shape, own.dtype)], (own, came))[0]


def passed_along(block, distance):
    devices = range(lax.axis_size("seq"))
    route = [(i - distance, i) for i in devices if i - distance in devices]
    return lax.ppermute(block, "seq", route)


def spread(block, level):
    count = lax.axis_size("seq")
    size = 2 << level
    arrived = []
    for turn in range(1 << level):
        route = []
        for base in range(0, count // 2, size):
            low, high = base + size // 2 - 1, base + size // 2
            for parity in range(2):
                route.append((2 * low + parity, 2 * (high + turn) + parity))
                route.append((2 * high + parity, 2 * (low - turn) + parity))
        arrived.append(lax.ppermute(block, "seq", route))
    return arrived


def levels():
    return (lax.axis_size("seq") // 2).bit_length() - 1


def upper(level):
    return ((lax.axis_index("seq") // 2) >> level) % 2 == 1


def sides(gots):
    low = high = None
    for level, arrived in enumerate(gots):
        got = sum(x[...].astype(F32) for x in arrived)
        above = upper(level)
        a, b = jnp.where(above, got, 0.0), jnp.where(above, 0.0, got)
        low, high = (a, b) if low is None else (low + a, high + b)
    return low, high


def by_level(refs):
    gots, at = [], 0
    while at < len(refs):
        count = 1 << len(gots)
        gots.append(refs[at : at + count])
        at += count
    return gots


def pair_kernel(kept, came, pair, send):
    total = kept[...].astype(F32) + came[...].astype(F32)
    pair[...] = total.astype(BF)
    send[...] = jnp.where(upper(0), total[1], total[0]).astype(BF)


def pair_sum(kept, came):
    return call(
        pair_kernel, "pair_sum", [array(kept.shape, BF), array(kept.shape[1:], BF)], (kept, came)
    )


def level_kernel(pair, *refs):
    *gots, send = refs
    gots = by_level(gots)
    low, high = sides(gots)
    above = upper(len(gots))
    send[...] = jnp.where(
        above, pair[1].astype(F32) + high, pair[0].astype(F32) + low
    ).astype(BF)


def level_sum(pair, gots):
    return call(level_kernel, "level_sum", [array(pair.shape[1:], BF)], (pair, *gots))[0]


def entering_kernel(kept, came, *refs):
    *gots, mine, others = refs
    low, high = sides(by_level(gots))
    zero = jnp.zeros_like(low)
    low, high = (zero, zero) if low is None else (low, high)
    first = own_half() == 0
    mine[0] = (low + jnp.where(first, zero, came[0].astype(F32))).astype(BF)
    mine[1] = (high + jnp.where(first, came[1].astype(F32), zero)).astype(BF)
    others[0] = (low + jnp.where(first, kept[0].astype(F32), zero)).astype(BF)
    others[1] = (high + jnp.where(first, zero, kept[1].astype(F32))).astype(BF)


def entering(kept, came, gots):
    return call(
        entering_kernel, "entering", [array(kept.shape, BF)] * 2, (kept, came, *gots)
    )


def near_kernel(keep, came, mine, a, b, c):
    def total(side, y):
        return keep[side, y].astype(F32) + came[side, y].astype(F32)

    mine[...] = total(0, 0)
    a[...], b[...], c[...] = (total(*at).astype(BF) for at in ((1, 0), (0, 1), (1, 1)))


def near_sum(keep, came):
    part = array(keep.shape[2:], BF)
    return call(
        near_kernel, "near_sum", [array(part.shape, F32), part, part, part], (keep, came)
    )


def total_kernel(count, *refs):
    refs[-1][...] = sum(x[...].astype(F32) for x in refs[:count]).astype(BF)


def total_of(arrays, follows=()):
    return call(
        functools.partial(total_kernel, len(arrays)),
        "total",
        [array(arrays[0].shape, BF)],
        (*arrays, *follows),
        unread=len(follows),
    )[0]


def assemble_kernel(norm, *refs):
    pieces, out = refs[:-1], refs[-1]
    core, far = lax.axis_index("dp") % 2, lax.axis_index("dp") // 2
    for side in range(2):
        half = own_half() ^ side
        for n in range(CHUNKS):
            for c in range(2):
                for y in range(2):
                    head = half * HALF + n * CHUNK + (c ^ core) * 2 + (y ^ far)
                    out[head] = pieces[side * 4 + c * 2 + y][n].astype(F32) * norm


def assemble(pieces, norm):
    return call(
        functools.partial(assemble_kernel, norm), "assemble", [array((HEADS, HD, HD), F32)], pieces
    )[0]


def on_device(
    linear_queries, linear_keys, window_queries, window_keys, values, cotangent, feature_map
):
    tokens = linear_queries.shape[1]
    total_tokens = tokens * lax.axis_size("seq") * lax.axis_size("dp") * linear_queries.shape[0]
    lq, lk, wq, wk, v, g = (
        x[0]
        for x in (linear_queries, linear_keys, window_queries, window_keys, values, cotangent)
    )
    rows = (lq, lk, v, g)
    inputs = (*rows, feature_map, wk)
    fq_o, fk_o, *given, ends = features(*inputs, None)
    came = [flipped(x, 1) for x in given]
    far_ends = relayed(ends)
    fq, fk, *kept = features(*inputs, fq_o)
    came[-1], far_ends = lax.optimization_barrier((came[-1], far_ends))
    rims = flipped(relay(ends, far_ends), 1)
    pair, sent = zip(*(pair_sum(a, b) for a, b in zip(kept, came)))
    pair, sent = list(pair), list(sent)
    gots = [[] for _ in range(CHUNKS)]
    for level in range(levels()):
        if level > 0:
            sent = [level_sum(pair[n], gots[n]) for n in range(CHUNKS)]
        for n in range(CHUNKS):
            gots[n] += spread(sent[n], level)
    mine, others = zip(*(entering(kept[n], came[n], gots[n]) for n in range(CHUNKS)))
    back = [flipped(x, 1) for x in others]
    *windows, edge = window_part(wq, wk, v, g, rims, others[-1])
    dpq, dpk, *terms = state_part(0, CHUNKS, (*rows, fq, fk), mine, (), (others[-1],))
    own = (*mine, fq, fk, dpq, dpk)
    back[0], edge, terms = lax.optimization_barrier((back[0], edge, terms))
    edge = passed_along(edge, -1)
    pairs = [None] * CHUNKS
    for n in reversed(range(CHUNKS)):
        *pairs[n], keep, send = state_part(n, 1, (*rows, fq_o, fk_o), (back[n],), terms)
        terms = (keep, send)
    other = (*back, fq_o, fk_o, *(x for pair in pairs for x in pair))
    keep, send = terms
    near, a, b, c = near_sum(keep, flat_flipped(send, 0, 1))
    a, b, c = flat_flipped(a, 1, 0), flat_flipped(b, 0, 2), flat_flipped(c, 1, 2)
    sent = total_of((near, a, b, c))
    came = [flat_flipped(sent, bits, 0) for bits in range(2, lax.axis_size("seq"), 2)]
    attended, dlq, dlk, dv, dwq, dwk, token = output_part(
        v, g, feature_map, (*windows, edge), own, other
    )
    done = total_of((sent, *came), (token,))
    a, b, c = flat_flipped(done, 1, 0), flat_flipped(done, 0, 2), flat_flipped(done, 1, 2)
    across = [flat_flipped(x, 0, 1) for x in (done, b, a, c)]
    map_grad = assemble(
        (done, b, *across[:2], a, c, *across[2:]), total_tokens ** (-0.5)
    )
    return attended[None], dlq[None], dlk[None], dwq[None], dwk[None], dv[None], map_grad


def solution(mesh):
    row = P("dp", "seq", None)
    return jax.shard_map(
        on_device,
        mesh=mesh,
        in_specs=(row,) * 6 + (P(),),
        out_specs=(row,) * 6 + (P(),),
        check_vma=False,
    )
```
